256 devices in a mesh: lon: 64 (over y, x_hi, z), lat: 4 (over x_lo, core).
Axes of the slice: x: 4 (x_hi: 2, x_lo: 2; x = x_hi * 2 + x_lo), y: 4, z: 8, core: 2. Of those that a mesh axis runs over, the one named last changes fastest.
Arguments:
- queries: bfloat16 [64, 1024, 1024], P('lat', 'lon'), may hold values from -8 to 8
- key_vectors: bfloat16 [64, 1024, 1024], P('lat', 'lon'), may hold values from -8 to 8
- value_vectors: bfloat16 [64, 1024, 1024], P('lat', 'lon'), may hold values from -6 to 6
- grad_out: bfloat16 [64, 1024, 1024], P('lat', 'lon'), may hold values from -6 to 6
- key_mask: int32 [64, 1024], P('lat', 'lon'), may hold values 0 or 1
- block_lists: int32 [64, 3], P('lon'), may hold values from 0 to 63, as said below
Outputs:
- attended: bfloat16 [64, 1024, 1024], P('lat', 'lon')
- grad_queries: bfloat16 [64, 1024, 1024], P('lat', 'lon')
- grad_keys: bfloat16 [64, 1024, 1024], P('lat', 'lon')
- grad_values: bfloat16 [64, 1024, 1024], P('lat', 'lon')
The draws below stay inside these ranges and needn't reach their ends.
Inputs may be any that keep to these rules, and one draw needn't show every extreme that they name: `block_lists`: row b names 3 different blocks: b itself, one block exactly 3 blocks from b around the loop of 64 blocks, and one block nearer to b than that, in any order.
All inputs are finite; a program needn't handle non-finite values. No bound on the sum of `key_mask` on one device may be relied on, other than what follows from the above.
Results may differ from the reference program's by a relative error of at most 0.013.
The reference program's roundings to bfloat16 on the way count: a program that leaves them out, or rounds other values in their place, can miss the bound.
Values may be sent and summed in bfloat16 or wider, within the bound.
A program may use at most 128 MiB of HBM per device.

```python
import jax
import jax.numpy as jnp
from jax import lax

HEAD = 64
NB_HEADS = 12
CH = 1024
RAD = 6
RANGE = 3
NSRC = 3
LON_DEV = 16
NLAT = 64
NLON = 1024
NBLK = 64


def draw_queries(key, part):
    key = jax.random.fold_in(key, 11)
    return jnp.clip(jax.random.normal(key, (NLAT, NLON, CH), jnp.float32), -8.0, 8.0).astype(jnp.bfloat16)


def draw_key_vectors(key, part):
    key = jax.random.fold_in(key, 23)
    return jnp.clip(jax.random.normal(key, (NLAT, NLON, CH), jnp.float32), -8.0, 8.0).astype(jnp.bfloat16)


def draw_block_lists(key, part):
    key = jax.random.fold_in(key, 5)
    first, second, third, fourth = jax.random.split(key, 4)
    blocks = jnp.arange(NBLK, dtype=jnp.int32)
    far_sign = 2 * jax.random.randint(first, (NBLK,), 0, 2) - 1
    near_step = jax.random.randint(second, (NBLK,), 1, RANGE) * (2 * jax.random.randint(third, (NBLK,), 0, 2) - 1)
    table = jnp.stack([blocks, (blocks + far_sign * RANGE) % NBLK, (blocks + near_step) % NBLK], axis=1)
    ranks = jax.random.randint(fourth, (NBLK, NSRC), 0, 1024) * NSRC + jnp.arange(NSRC, dtype=jnp.int32)[None, :]
    order = jnp.argsort(ranks, axis=1)
    return jnp.take_along_axis(table, order, axis=1).astype(jnp.int32)


def with_ends(values, rng, low, top_value):
    longest = values.shape.index(max(values.shape))
    spots = []
    for shift in (0, 1):
        where = [jax.random.randint(jax.random.fold_in(rng, axis), (), 0, length) for axis, length in enumerate(values.shape)]
        where[longest] = (where[longest] + shift) % values.shape[longest]
        spots.append(tuple(where))
    return values.at[spots[0]].set(low).at[spots[1]].set(top_value)


def block_levels(stream_key, extent, pieces, smallest, top_value):
    level, own = 1.0, jax.random.fold_in(stream_key, 6)
    for dim, shards_of in pieces:
        heights = jnp.exp(jax.random.uniform(jax.random.fold_in(own, dim), (shards_of,), jnp.float32, smallest / len(pieces), top_value / len(pieces)))
        level = level * jnp.repeat(heights, extent[dim] // shards_of).reshape([-1 if axis == dim else 1 for axis in range(len(extent))])
    return level


def normal_values(stream_key, dims, spread, limit, shards=(), held_as=jnp.bfloat16):
    array = spread * jax.random.normal(stream_key, dims, jnp.float32)
    if shards:
        array = array * block_levels(stream_key, dims, shards, -0.22, 0.18)
    return jnp.clip(array, -limit, limit).astype(held_as)


def setup_inputs(seed: int = 0) -> dict:
    splits = jax.random.split(jax.random.key(seed), 7)
    queries = draw_queries(jax.random.fold_in(splits[6], 71), 0)
    key_vectors = draw_key_vectors(jax.random.fold_in(splits[6], 71), 0)
    value_vectors = normal_values(splits[2], (NLAT, NLON, CH), 1.0, 6.0, ((0, 4), (1, 64)))
    grad_out = normal_values(splits[3], (NLAT, NLON, CH), 1.0, 6.0, ((0, 4), (1, 64)))
    key_mask = with_ends((jax.random.randint(splits[4], (NLAT, NLON), 0, 8) < 7).astype(jnp.int32), jax.random.fold_in(splits[4], 1), 0, 1)
    block_lists = draw_block_lists(jax.random.fold_in(splits[6], 71), 0)
    return {"queries": queries, "key_vectors": key_vectors, "value_vectors": value_vectors, "grad_out": grad_out, "key_mask": key_mask, "block_lists": block_lists}


NEG = -1e30


def rounded(field):
    return lax.optimization_barrier(field.astype(jnp.bfloat16)).astype(jnp.float32)


def wrap_pad(field):
    field = jnp.concatenate([field[:, -RAD:], field, field[:, :RAD]], axis=1)
    widths = [(RAD, RAD)] + [(0, 0)] * (field.ndim - 1)
    return jnp.pad(field, widths)


def fold_back(padded, rows):
    core = padded[RAD:RAD + rows]
    middle = core[:, RAD:-RAD]
    middle = middle.at[:, :RAD].add(core[:, -RAD:])
    middle = middle.at[:, -RAD:].add(core[:, :RAD])
    return middle


def window_part(queries, keys, values, grad_out, key_mask):
    rows, cols, chans = queries.shape
    heads = chans // HEAD
    scale = HEAD ** -0.5
    span = 2 * RAD + 1
    key_pad = wrap_pad(keys)
    value_pad = wrap_pad(values)
    mask_pad = wrap_pad((key_mask > 0).astype(jnp.int32))
    query_f = queries.astype(jnp.float32).reshape(rows, cols, heads, HEAD)
    grad_f = grad_out.astype(jnp.float32).reshape(rows, cols, heads, HEAD)
    offsets = jnp.arange(span * span, dtype=jnp.int32)
    centre = RAD * span + RAD
    zero = jnp.int32(0)

    def cut(field, index):
        start = (index // span, index % span) + (zero,) * (field.ndim - 2)
        return lax.dynamic_slice(field, start, (rows, cols) + field.shape[2:])

    def scored(index):
        shifted = cut(key_pad, index).astype(jnp.float32).reshape(rows, cols, heads, HEAD)
        scores = jnp.sum(query_f * shifted, axis=-1) * scale
        admit = (cut(mask_pad, index) > 0) | (index == centre)
        return scores, admit[:, :, None], shifted

    def moved_values(index):
        return cut(value_pad, index).astype(jnp.float32).reshape(rows, cols, heads, HEAD)

    def step_max(maxima, index):
        scores, admit, shifted = scored(index)
        return jnp.maximum(maxima, jnp.where(admit, scores, NEG)), None

    maxima, _ = lax.scan(step_max, jnp.full((rows, cols, heads), NEG, jnp.float32), offsets)

    def step_total(totals, index):
        scores, admit, shifted = scored(index)
        return totals + jnp.where(admit, jnp.exp(scores - maxima), 0.0), None

    totals, _ = lax.scan(step_total, jnp.zeros((rows, cols, heads), jnp.float32), offsets)

    def step_out(summed, index):
        scores, admit, shifted = scored(index)
        probs = rounded(jnp.where(admit, jnp.exp(scores - maxima), 0.0) / totals)
        return summed + probs[..., None] * moved_values(index), None

    summed, _ = lax.scan(step_out, jnp.zeros((rows, cols, heads, HEAD), jnp.float32), offsets)
    attended = summed.astype(jnp.bfloat16)
    logsum = maxima + jnp.log(totals)
    delta = jnp.sum(grad_f * attended.astype(jnp.float32), axis=-1)

    def step_back(carry, index):
        grad_q, grad_k, grad_v = carry
        scores, admit, shifted = scored(index)
        back = jnp.where(admit, jnp.exp(scores - logsum), 0.0)
        dprob = jnp.sum(grad_f * moved_values(index), axis=-1)
        dscore = rounded(back * (dprob - delta))
        weights = rounded(back)
        grad_q = grad_q + dscore[..., None] * shifted
        start = (index // span, index % span, zero, zero)
        size = (rows, cols, heads, HEAD)
        grad_k = lax.dynamic_update_slice(grad_k, lax.dynamic_slice(grad_k, start, size) + dscore[..., None] * query_f, start)
        grad_v = lax.dynamic_update_slice(grad_v, lax.dynamic_slice(grad_v, start, size) + weights[..., None] * grad_f, start)
        return (grad_q, grad_k, grad_v), None

    padded_zero = jnp.zeros((rows + 2 * RAD, cols + 2 * RAD, heads, HEAD), jnp.float32)
    start_carry = (jnp.zeros((rows, cols, heads, HEAD), jnp.float32), padded_zero, padded_zero)
    (grad_q, grad_k, grad_v), _ = lax.scan(step_back, start_carry, offsets)
    grad_queries = (grad_q * scale).reshape(rows, cols, chans).astype(jnp.bfloat16)
    grad_keys = (fold_back(grad_k, rows) * scale).reshape(rows, cols, chans).astype(jnp.bfloat16)
    grad_values = fold_back(grad_v, rows).reshape(rows, cols, chans).astype(jnp.bfloat16)
    return attended.reshape(rows, cols, chans), grad_queries, grad_keys, grad_values


def axial_part(queries, keys, values, grad_out, key_mask, block_lists):
    rows, cols, chans = queries.shape
    heads = chans // HEAD
    blocks = cols // LON_DEV
    scale = HEAD ** -0.5
    width = NSRC * LON_DEV
    shape_five = (rows, blocks, LON_DEV, heads, HEAD)
    query_f = queries.astype(jnp.float32).reshape(shape_five)
    key_f = keys.astype(jnp.float32).reshape(shape_five)
    value_f = values.astype(jnp.float32).reshape(shape_five)
    grad_f = grad_out.astype(jnp.float32).reshape(shape_five)
    mask_flag = (key_mask > 0).reshape(rows, blocks, LON_DEV)
    column = jnp.arange(LON_DEV, dtype=jnp.int32)
    diagonal_cells = column[:, None] == column[None, :]

    def per_block(carry, block):
        grad_k, grad_v = carry
        listed = block_lists[block]
        own_q = query_f[:, block]
        own_g = grad_f[:, block]
        near_k = jnp.take(key_f, listed, axis=1).reshape(rows, width, heads, HEAD)
        near_v = jnp.take(value_f, listed, axis=1).reshape(rows, width, heads, HEAD)
        near_m = jnp.take(mask_flag, listed, axis=1).reshape(rows, width)
        same = (diagonal_cells[:, None, :] & (listed == block)[None, :, None]).reshape(LON_DEV, width)
        admit = (near_m[:, None, :] | same[None])[:, None]
        scores = jnp.einsum("aqhd,akhd->ahqk", own_q, near_k) * scale
        maxima = jnp.max(jnp.where(admit, scores, NEG), axis=-1)
        expo = jnp.where(admit, jnp.exp(scores - maxima[..., None]), 0.0)
        totals = jnp.sum(expo, axis=-1)
        probs = rounded(expo / totals[..., None])
        attended = jnp.einsum("ahqk,akhd->aqhd", probs, near_v).astype(jnp.bfloat16)
        logsum = maxima + jnp.log(totals)
        delta = jnp.einsum("aqhd,aqhd->ahq", own_g, attended.astype(jnp.float32))
        back = jnp.where(admit, jnp.exp(scores - logsum[..., None]), 0.0)
        weights = rounded(back)
        dprob = jnp.einsum("aqhd,akhd->ahqk", own_g, near_v)
        dscore = rounded(back * (dprob - delta[..., None]))
        grad_q = (jnp.einsum("ahqk,akhd->aqhd", dscore, near_k) * scale).astype(jnp.bfloat16)
        part_k = (jnp.einsum("ahqk,aqhd->akhd", dscore, own_q) * scale).reshape(rows, NSRC, LON_DEV, heads, HEAD)
        part_v = jnp.einsum("ahqk,aqhd->akhd", weights, own_g).reshape(rows, NSRC, LON_DEV, heads, HEAD)
        for slot in range(NSRC):
            grad_k = grad_k.at[:, listed[slot]].add(part_k[:, slot])
            grad_v = grad_v.at[:, listed[slot]].add(part_v[:, slot])
        return (grad_k, grad_v), (attended, grad_q)

    zeros_five = jnp.zeros(shape_five, jnp.float32)
    (grad_k, grad_v), (attended, grad_q) = lax.scan(per_block, (zeros_five, zeros_five), jnp.arange(blocks, dtype=jnp.int32))
    attended = jnp.transpose(attended, (1, 0, 2, 3, 4)).reshape(rows, cols, chans)
    grad_q = jnp.transpose(grad_q, (1, 0, 2, 3, 4)).reshape(rows, cols, chans)
    grad_keys = grad_k.reshape(rows, cols, chans).astype(jnp.bfloat16)
    grad_values = grad_v.reshape(rows, cols, chans).astype(jnp.bfloat16)
    return attended, grad_q, grad_keys, grad_values


def reference(queries, key_vectors, value_vectors, grad_out, key_mask, block_lists):
    split = NB_HEADS * HEAD
    first = window_part(queries[..., :split], key_vectors[..., :split], value_vectors[..., :split], grad_out[..., :split], key_mask)
    second = axial_part(queries[..., split:], key_vectors[..., split:], value_vectors[..., split:], grad_out[..., split:], key_mask, block_lists)
    return (jnp.concatenate([first[0], second[0]], axis=-1), jnp.concatenate([first[1], second[1]], axis=-1), jnp.concatenate([first[2], second[2]], axis=-1), jnp.concatenate([first[3], second[3]], axis=-1))
```

```python
import functools

import jax
import jax.numpy as jnp
import numpy as np
from jax import lax
from jax.experimental import pallas as pl
from jax.experimental.pallas import tpu as pltpu
from jax.sharding import PartitionSpec as P

HEAD = 64
NB_HEADS = 12
RAD = 6
RANGE = 3
SIDE = 16
CELLS = SIDE * SIDE
WCH = NB_HEADS * HEAD
PAIR = 2 * HEAD
PAIRS = WCH // PAIR
XPAIRS = 2
STRIP = RAD * SIDE
LEFT = CELLS
RIGHT = CELLS + STRIP
EDGE = CELLS + 2 * STRIP
CORNER = EDGE + STRIP
KEYS = CORNER + STRIP
NSLOT = 2 * RANGE + 1
GROUP = 64
GROUPS = CELLS // GROUP
NEG = -1e30
SCALE = HEAD**-0.5
BF = jnp.bfloat16
F32 = jnp.float32
NEAR = [(o, 0) for o in (1, -1, 2, -2, 3, -3)] + [(o, a) for a in (-1, 1) for o in (0, 1, -1)]


def key_places(tile):
    rows = np.full(KEYS, 1000)
    cols = np.full(KEYS, 1000)
    own = np.arange(CELLS)
    rows[:CELLS], cols[:CELLS] = own // SIDE, own % SIDE
    strip = np.arange(STRIP)
    rows[LEFT:RIGHT], cols[LEFT:RIGHT] = strip % SIDE, strip // SIDE - RAD
    rows[RIGHT:EDGE], cols[RIGHT:EDGE] = strip % SIDE, strip // SIDE + SIDE
    first = -RAD if tile == 0 else SIDE
    rows[EDGE:CORNER], cols[EDGE:CORNER] = first + strip // SIDE, strip % SIDE
    for side in range(2):
        for c in range(RAD):
            for r in range(RAD):
                at = CORNER + side * RAD * RAD + c * RAD + r
                rows[at] = first + r
                cols[at] = c - RAD if side == 0 else c + SIDE
    return rows, cols


def tables():
    window = np.zeros((2, KEYS, 128), np.float32)
    lane = np.arange(128)
    for tile in range(2):
        rows, cols = key_places(tile)
        q_row, q_col = lane // SIDE + 8 * tile, lane % SIDE
        dr = rows[:, None] - q_row[None, :]
        dc = cols[:, None] - q_col[None, :]
        window[tile] = ((np.abs(dr) <= RAD) & (np.abs(dc) <= RAD)) + 1.0 * ((dr == 0) & (dc == 0))
    slot = np.arange(NSLOT * GROUP)
    cell = slot % GROUP
    query = lane % GROUP
    axial = (cell[:, None] // SIDE == query[None, :] // SIDE) + 1.0 * (
        (cell[:, None] == query[None, :]) & (slot[:, None] // GROUP == RANGE)
    )
    strips = np.zeros((2 * STRIP, CELLS), np.float32)
    for c in range(RAD):
        for r in range(SIDE):
            strips[c * SIDE + r, r * SIDE + SIDE - RAD + c] = 1
            strips[STRIP + c * SIDE + r, r * SIDE + c] = 1
    corners = np.zeros((2 * STRIP, 2 * STRIP), np.float32)
    for side in range(2):
        for c in range(RAD):
            for r in range(RAD):
                at = side * RAD * RAD + c * RAD + r
                corners[at, side * STRIP + c * SIDE + r] = 1
                corners[STRIP + at, side * STRIP + c * SIDE + SIDE - RAD + r] = 1
    return [jnp.asarray(t, BF) for t in (window, axial, strips, strips.T, corners, corners.T)]


def mm(a, b):
    return jnp.dot(a, b, preferred_element_type=F32)


def mm_nt(a, b):
    return lax.dot_general(a, b, (((1,), (1,)), ((), ())), preferred_element_type=F32)


def mm_tn(a, b):
    return lax.dot_general(a, b, (((0,), (0,)), ((), ())), preferred_element_type=F32)


def stacked_heads(block):
    low = lax.broadcasted_iota(jnp.int32, block.shape, 1) < HEAD
    zero = jnp.zeros_like(block)
    return jnp.concatenate([jnp.where(low, block, zero), jnp.where(low, zero, block)], axis=0)


def probabilities(scores, dprob):
    top = jnp.max(scores, axis=0, keepdims=True)
    expo = jnp.exp(scores - top)
    probs = expo * (1.0 / jnp.sum(expo, axis=0, keepdims=True))
    delta = jnp.sum(probs * dprob, axis=0, keepdims=True)
    return probs.astype(BF), (probs * (dprob - delta)).astype(BF)


def kernel(
    nlon, nlat,
    q_ref, k_ref, v_ref, g_ref, flag_ref, listed_ref,
    near_ref, row_ref, strips_ref, strips_t_ref, corners_ref, corners_t_ref,
    out_ref, gq_ref, gk_ref, gv_ref,
    flags, columns, bias, xbias, kv, strip_out, corner_out, xkv,
    acc, sides, edge_out, edge_in, side_out, side_in, gx, hop_out, hop_in,
    flag_s, flag_r, strip_s, strip_r, edge_s, edge_r, corner_s, corner_r, ax_s, ax_r,
    bedge_s, bedge_r, bside_s, bside_r, hop_s, hop_r,
):
    lon = lax.axis_index("lon")
    lat = lax.axis_index("lat")
    has_up = lat > 0
    has_down = lat < nlat - 1

    def device(dlon, dlat):
        return {"lon": lax.rem(lon + dlon + nlon, nlon), "lat": lax.rem(lat + dlat + nlat, nlat)}

    def remote(src, dst, send, recv, dlon, dlat):
        return pltpu.make_async_remote_copy(
            src_ref=src, dst_ref=dst, send_sem=send, recv_sem=recv,
            device_id=device(dlon, dlat), device_id_type=pl.DeviceIdType.MESH,
        )

    barrier = pltpu.get_barrier_semaphore()
    for dlon, dlat in NEAR:
        pl.semaphore_signal(barrier, inc=1, device_id=device(dlon, dlat), device_id_type=pl.DeviceIdType.MESH)

    flags[RANGE] = flag_ref[...]
    for part, ref in enumerate((k_ref, v_ref)):
        cells = ref[:, :WCH]
        for tile in range(2):
            kv[tile, part, 0:CELLS] = cells
        strip_out[part] = mm(strips_ref[...], cells).astype(BF)
        for pair in range(XPAIRS):
            at = (2 * pair + part) * PAIR
            xkv[RANGE, :, at:at + PAIR] = ref[:, WCH + pair * PAIR:WCH + (pair + 1) * PAIR]
    for tile, there in enumerate((has_up, has_down)):
        @pl.when(jnp.logical_not(there))
        def _():
            kv[tile, :, EDGE:KEYS] = jnp.zeros((2, KEYS - EDGE, WCH), BF)
            edge_in[tile] = jnp.zeros(edge_in.shape[1:], BF)

    pl.semaphore_wait(barrier, len(NEAR))

    def flag_copy(index):
        dlon, dlat = NEAR[index]
        slot = {0: RANGE, -1: 11, 1: 8}[dlat] - dlon
        return remote(flags.at[RANGE], flags.at[slot], flag_s.at[index], flag_r.at[slot], dlon, dlat)

    def strip_copy(way):
        return remote(
            strip_out.at[:, pl.ds(way * STRIP, STRIP)], kv.at[0, :, pl.ds(LEFT + way * STRIP, STRIP)],
            strip_s.at[way], strip_r.at[way], 1 - 2 * way, 0,
        )

    def edge_copy(way):
        return remote(
            kv.at[0, :, pl.ds(way * (CELLS - STRIP), STRIP)], kv.at[1 - way, :, pl.ds(EDGE, STRIP)],
            edge_s.at[way], edge_r.at[way], 0, 2 * way - 1,
        )

    def corner_copy(way):
        return remote(
            corner_out.at[:, pl.ds(way * STRIP, STRIP)], kv.at[1 - way, :, pl.ds(CORNER, STRIP)],
            corner_s.at[way], corner_r.at[way], 0, 2 * way - 1,
        )

    def ax_copy(way, step):
        sign = 1 - 2 * way
        return remote(
            xkv.at[RANGE - sign * step], xkv.at[RANGE - sign * (step + 1)],
            ax_s.at[way, step], ax_r.at[way, step], sign, 0,
        )

    def edge_back(way, pair):
        lanes = pl.ds(pl.multiple_of(pair * PAIR, PAIR), PAIR)
        return remote(
            edge_out.at[way, :, :, lanes], edge_in.at[1 - way, :, :, lanes],
            bedge_s.at[way, pair], bedge_r.at[way, pair], 0, 2 * way - 1,
        )

    def side_back(way, pair):
        lanes = pl.ds(pl.multiple_of(pair * PAIR, PAIR), PAIR)
        rows = pl.ds(way * STRIP, STRIP)
        return remote(
            side_out.at[:, rows, lanes], side_in.at[:, rows, lanes],
            bside_s.at[way, pair], bside_r.at[way, pair], 2 * way - 1, 0,
        )

    def hop_back(way, step, pair):
        lanes = pl.ds(pair * 2 * PAIR, 2 * PAIR)
        return remote(
            hop_out.at[way, step, :, lanes], hop_in.at[way, step, :, lanes],
            hop_s.at[way, step, pair], hop_r.at[way, step, pair], 1 - 2 * way, 0,
        )

    def vertical(make, sending):
        @pl.when(has_up)
        def _():
            make(0 if sending else 1)

        @pl.when(has_down)
        def _():
            make(1 if sending else 0)

    for index in range(len(NEAR)):
        flag_copy(index).start()
    for way in range(2):
        strip_copy(way).start()
    vertical(lambda way: edge_copy(way).start(), True)
    for way in range(2):
        ax_copy(way, 0).start()

    for index in range(len(NEAR)):
        flag_copy(index).wait_recv()
    for slot in range(13):
        for half in range(2):
            row = jnp.broadcast_to(flags[slot, half:half + 1, :], (128, 128))
            columns[slot, half * 128:(half + 1) * 128] = row.T.astype(BF)

    def sides_of(left, right):
        return jnp.concatenate(
            [mm(strips_ref[0:STRIP], columns[left]), mm(strips_ref[STRIP:], columns[right])], axis=0
        )

    own_flags = columns[RANGE].astype(F32)
    side_flags = sides_of(RANGE - 1, RANGE + 1)
    for tile, there in enumerate((has_up, has_down)):
        base = 7 + 3 * tile
        lives = jnp.where(there, 1.0, 0.0)
        first = CELLS - STRIP if tile == 0 else 0
        edge_flags = columns[base + 1, first:first + STRIP].astype(F32)
        turn = corners_ref[STRIP:] if tile == 0 else corners_ref[0:STRIP]
        corner_flags = mm(turn, sides_of(base, base + 2).astype(BF))
        serves = jnp.concatenate([own_flags, side_flags, edge_flags * lives, corner_flags * lives], axis=0)
        bias[tile] = jnp.where(near_ref[tile].astype(F32) + serves > 1.5, 0.0, NEG)
    for group in range(GROUPS):
        serves = jnp.concatenate(
            [
                columns[slot, group * GROUP:(group + 1) * GROUP].astype(F32) * listed_ref[slot:slot + 1, :]
                for slot in range(NSLOT)
            ],
            axis=0,
        )
        xbias[group] = jnp.where(row_ref[...].astype(F32) + serves > 1.5, 0.0, NEG)

    for way in range(2):
        strip_copy(way).wait_recv()
    for part in range(2):
        strip = kv[0, part, LEFT:EDGE]
        kv[1, part, LEFT:EDGE] = strip
        corner_out[part] = mm(corners_ref[...], strip).astype(BF)
    vertical(lambda way: corner_copy(way).start(), True)
    vertical(lambda way: edge_copy(way).wait_recv(), False)
    vertical(lambda way: corner_copy(way).wait_recv(), False)

    def send_sides(pair):
        lanes = pl.ds(pl.multiple_of(pair * PAIR, PAIR), PAIR)
        vertical(lambda way: edge_back(way, pair).wait_recv(), False)
        for part in range(2):
            found = jnp.concatenate(
                [edge_in[0, part, STRIP:2 * STRIP, lanes], edge_in[1, part, STRIP:2 * STRIP, lanes]], axis=0
            )
            side_out[part, :, lanes] = (sides[part, :, lanes] + mm(corners_t_ref[...], found)).astype(BF)
        for way in range(2):
            side_back(way, pair).start()

    def window_pair(pair, carry):
        lanes = pl.ds(pl.multiple_of(pair * PAIR, PAIR), PAIR)
        grads = []
        for tile in range(2):
            rows = slice(tile * 128, (tile + 1) * 128)
            queries = stacked_heads(q_ref[rows, lanes] * jnp.asarray(SCALE, BF))
            cotangents = stacked_heads(g_ref[rows, lanes])
            keys = kv[tile, 0, :, lanes]
            values = kv[tile, 1, :, lanes]
            penalty = bias[tile]
            scores = mm_nt(keys, queries) + jnp.concatenate([penalty, penalty], axis=1)
            probs, dscore = probabilities(scores, mm_nt(values, cotangents))
            attended = mm_tn(values, probs)
            grad_q = mm_tn(keys, dscore)
            for result, ref, factor in ((attended, out_ref, 1.0), (grad_q, gq_ref, SCALE)):
                both = jnp.concatenate([result[0:HEAD, 0:128], result[HEAD:, 128:]], axis=0)
                ref[rows, lanes] = (both.T * factor).astype(BF)
            grads.append((mm(dscore, queries), mm(probs, cotangents)))
        for part in range(2):
            first, second = grads[0][part], grads[1][part]
            acc[part, :, lanes] = first[0:CELLS] + second[0:CELLS]
            sides[part, :, lanes] = first[LEFT:EDGE] + second[LEFT:EDGE]
            edge_out[0, part, :, lanes] = first[EDGE:].astype(BF)
            edge_out[1, part, :, lanes] = second[EDGE:].astype(BF)
        vertical(lambda way: edge_back(way, pair).start(), True)

        for step in range(2):
            @pl.when(pair == 2 * step + 1)
            def _():
                for way in range(2):
                    ax_copy(way, step).wait_recv()
                    ax_copy(way, step + 1).start()

        @pl.when(pair > 0)
        def _():
            send_sides(pair - 1)

        return carry

    lax.fori_loop(0, PAIRS, window_pair, 0)
    send_sides(PAIRS - 1)
    for way in range(2):
        ax_copy(way, 2).wait_recv()

    for pair in range(XPAIRS):
        lanes = slice(WCH + pair * PAIR, WCH + (pair + 1) * PAIR)
        key_lanes = slice(2 * pair * PAIR, (2 * pair + 1) * PAIR)
        value_lanes = slice((2 * pair + 1) * PAIR, (2 * pair + 2) * PAIR)

        def axial_group(group, carry):
            cells = pl.ds(pl.multiple_of(group * GROUP, GROUP), GROUP)
            queries = stacked_heads(q_ref[cells, lanes] * jnp.asarray(SCALE, BF))
            cotangents = stacked_heads(g_ref[cells, lanes])
            keys = xkv[:, cells, key_lanes].reshape(NSLOT * GROUP, PAIR)
            values = xkv[:, cells, value_lanes].reshape(NSLOT * GROUP, PAIR)
            scores = mm_nt(keys, queries) + xbias[group]
            probs, dscore = probabilities(scores, mm_nt(values, cotangents))
            attended = mm_tn(probs, values)
            grad_q = mm_tn(dscore, keys)
            low = lax.broadcasted_iota(jnp.int32, (GROUP, PAIR), 1) < HEAD
            out_ref[cells, lanes] = jnp.where(low, attended[0:GROUP], attended[GROUP:]).astype(BF)
            gq_ref[cells, lanes] = (jnp.where(low, grad_q[0:GROUP], grad_q[GROUP:]) * SCALE).astype(BF)
            gx[:, cells, key_lanes] = mm(dscore, queries).reshape(NSLOT, GROUP, PAIR)
            gx[:, cells, value_lanes] = mm(probs, cotangents).reshape(NSLOT, GROUP, PAIR)
            return carry

        lax.fori_loop(0, GROUPS, axial_group, 0)
        both = slice(2 * pair * PAIR, (2 * pair + 2) * PAIR)
        for way in range(2):
            hop_out[way, 0, :, both] = gx[2 * RANGE * (1 - way), :, both].astype(BF)
            hop_back(way, 0, pair).start()

    for step in range(1, RANGE):
        for pair in range(XPAIRS):
            both = slice(2 * pair * PAIR, (2 * pair + 2) * PAIR)
            for way in range(2):
                slot = 2 * RANGE - step if way == 0 else step
                hop_back(way, step - 1, pair).wait_recv()
                total = gx[slot, :, both] + hop_in[way, step - 1, :, both].astype(F32)
                hop_out[way, step, :, both] = total.astype(BF)
                hop_back(way, step, pair).start()

    for pair in range(PAIRS):
        for way in range(2):
            side_back(way, pair).wait_recv()
    for part, ref in enumerate((gk_ref, gv_ref)):
        total = acc[part] + mm(strips_t_ref[...], side_in[part])
        ref[0:STRIP, :WCH] = (total[0:STRIP] + edge_in[0, part, 0:STRIP].astype(F32)).astype(BF)
        ref[STRIP:CELLS - STRIP, :WCH] = total[STRIP:CELLS - STRIP].astype(BF)
        ref[CELLS - STRIP:, :WCH] = (total[CELLS - STRIP:] + edge_in[1, part, 0:STRIP].astype(F32)).astype(BF)

    for pair in range(XPAIRS):
        lanes = slice(WCH + pair * PAIR, WCH + (pair + 1) * PAIR)
        for way in range(2):
            hop_back(way, RANGE - 1, pair).wait_recv()
        for part, ref in enumerate((gk_ref, gv_ref)):
            at = slice((2 * pair + part) * PAIR, (2 * pair + part + 1) * PAIR)
            total = gx[RANGE, :, at]
            for way in range(2):
                total = total + hop_in[way, RANGE - 1, :, at].astype(F32)
            ref[:, lanes] = total.astype(BF)

    for index in range(len(NEAR)):
        flag_copy(index).wait_send()
    for way in range(2):
        strip_copy(way).wait_send()
        for step in range(RANGE):
            ax_copy(way, step).wait_send()
            for pair in range(XPAIRS):
                hop_back(way, step, pair).wait_send()
        for pair in range(PAIRS):
            side_back(way, pair).wait_send()
    vertical(lambda way: edge_copy(way).wait_send(), True)
    vertical(lambda way: corner_copy(way).wait_send(), True)
    for pair in range(PAIRS):
        vertical(lambda way: edge_back(way, pair).wait_send(), True)


def per_device(nlon, nlat, queries, key_vectors, value_vectors, grad_out, key_mask, block_lists):
    shape = queries.shape
    flat = [x.reshape(CELLS, shape[-1]) for x in (queries, key_vectors, value_vectors, grad_out)]
    flag = jnp.pad((key_mask > 0).astype(F32).reshape(2, 128), ((0, 6), (0, 0)))
    offset = (block_lists[0] - lax.axis_index("lon") + RANGE + nlon) % nlon
    listed = jnp.any(jnp.arange(8)[:, None] == offset[None, :], axis=1)
    listed = jnp.broadcast_to(listed[:, None], (8, 128)).astype(F32)
    vmem = pl.BlockSpec(memory_space=pltpu.VMEM)
    dma = lambda *s: pltpu.SemaphoreType.DMA(s)
    outs = pl.pallas_call(
        functools.partial(kernel, nlon, nlat),
        out_shape=[jax.ShapeDtypeStruct((CELLS, shape[-1]), BF)] * 4,
        in_specs=[vmem] * 12,
        out_specs=[vmem] * 4,
        scratch_shapes=[
            pltpu.VMEM((13, 8, 128), F32),
            pltpu.VMEM((13, CELLS, 128), BF),
            pltpu.VMEM((2, KEYS, 128), F32),
            pltpu.VMEM((GROUPS, NSLOT * GROUP, 128), F32),
            pltpu.VMEM((2, 2, KEYS, WCH), BF),
            pltpu.VMEM((2, 2 * STRIP, WCH), BF),
            pltpu.VMEM((2, 2 * STRIP, WCH), BF),
            pltpu.VMEM((NSLOT, CELLS, 2 * XPAIRS * PAIR), BF),
            pltpu.VMEM((2, CELLS, WCH), F32),
            pltpu.VMEM((2, 2 * STRIP, WCH), F32),
            pltpu.VMEM((2, 2, 2 * STRIP, WCH), BF),
            pltpu.VMEM((2, 2, 2 * STRIP, WCH), BF),
            pltpu.VMEM((2, 2 * STRIP, WCH), BF),
            pltpu.VMEM((2, 2 * STRIP, WCH), BF),
            pltpu.VMEM((NSLOT, CELLS, 2 * XPAIRS * PAIR), F32),
            pltpu.VMEM((2, RANGE, CELLS, 2 * XPAIRS * PAIR), BF),
            pltpu.VMEM((2, RANGE, CELLS, 2 * XPAIRS * PAIR), BF),
            dma(len(NEAR)), dma(13), dma(2), dma(2), dma(2), dma(2), dma(2), dma(2),
            dma(2, RANGE), dma(2, RANGE), dma(2, PAIRS), dma(2, PAIRS), dma(2, PAIRS), dma(2, PAIRS),
            dma(2, RANGE, XPAIRS), dma(2, RANGE, XPAIRS),
        ],
        compiler_params=pltpu.CompilerParams(
            collective_id=0, has_side_effects=True, vmem_limit_bytes=52 * 1024 * 1024
        ),
        cost_estimate=pl.CostEstimate(flops=4_000_000_000, bytes_accessed=5_000_000, transcendentals=3_000_000),
    )(*flat, flag, listed, *tables())
    return tuple(x.reshape(shape) for x in outs)


def solution(mesh):
    cells = P("lat", "lon", None)
    return jax.shard_map(
        functools.partial(per_device, mesh.shape["lon"], mesh.shape["lat"]),
        mesh=mesh,
        in_specs=(cells, cells, cells, cells, P("lat", "lon"), P("lon", None)),
        out_specs=(cells, cells, cells, cells),
        check_vma=False,
    )
```

```python
import functools

import jax
import jax.numpy as jnp
import numpy as np
from jax import lax
from jax.experimental import pallas as pl
from jax.experimental.pallas import tpu as pltpu
from jax.sharding import PartitionSpec as P

HEAD = 64
NB_HEADS = 12
RAD = 6
RANGE = 3
SIDE = 16
CELLS = SIDE * SIDE
WCH = NB_HEADS * HEAD
PAIR = 2 * HEAD
PAIRS = WCH // PAIR
XPAIRS = 2
STRIP = RAD * SIDE
LEFT = CELLS
RIGHT = CELLS + STRIP
EDGE = CELLS + 2 * STRIP
CORNER = EDGE + STRIP
KEYS = CORNER + STRIP
NSLOT = 2 * RANGE + 1
GROUP = 64
TURN = 80
LAG = 2
PIECES = 3
WIDE = WCH // PIECES
GROUPS = CELLS // GROUP
NEG = -1e30
SCALE = HEAD**-0.5
BF = jnp.bfloat16
F32 = jnp.float32
NEAR = [(o, 0) for o in (1, -1, 2, -2, 3, -3)] + [(o, a) for a in (-1, 1) for o in (0, 1, -1)]


def key_places(tile):
    rows = np.full(KEYS, 1000)
    cols = np.full(KEYS, 1000)
    own = np.arange(CELLS)
    rows[:CELLS], cols[:CELLS] = own // SIDE, own % SIDE
    strip = np.arange(STRIP)
    rows[LEFT:RIGHT], cols[LEFT:RIGHT] = strip % SIDE, strip // SIDE - RAD
    rows[RIGHT:EDGE], cols[RIGHT:EDGE] = strip % SIDE, strip // SIDE + SIDE
    first = -RAD if tile == 0 else SIDE
    rows[EDGE:CORNER], cols[EDGE:CORNER] = first + strip // SIDE, strip % SIDE
    for side in range(2):
        for c in range(RAD):
            for r in range(RAD):
                at = CORNER + side * RAD * RAD + c * RAD + r
                rows[at] = first + r
                cols[at] = c - RAD if side == 0 else c + SIDE
    return rows, cols


def tables():
    window = np.zeros((2, KEYS, 128), np.float32)
    lane = np.arange(128)
    for tile in range(2):
        rows, cols = key_places(tile)
        q_row, q_col = lane // SIDE + 8 * tile, lane % SIDE
        dr = rows[:, None] - q_row[None, :]
        dc = cols[:, None] - q_col[None, :]
        window[tile] = ((np.abs(dr) <= RAD) & (np.abs(dc) <= RAD)) + 1.0 * ((dr == 0) & (dc == 0))
    slot = np.arange(NSLOT * GROUP)
    cell = slot % GROUP
    query = lane % GROUP
    axial = (cell[:, None] // SIDE == query[None, :] // SIDE) + 1.0 * (
        (cell[:, None] == query[None, :]) & (slot[:, None] // GROUP == RANGE)
    )
    strips = np.zeros((2 * STRIP, CELLS), np.float32)
    for c in range(RAD):
        for r in range(SIDE):
            strips[c * SIDE + r, r * SIDE + SIDE - RAD + c] = 1
            strips[STRIP + c * SIDE + r, r * SIDE + c] = 1
    corners = np.zeros((2 * STRIP, 2 * STRIP), np.float32)
    for side in range(2):
        for c in range(RAD):
            for r in range(RAD):
                at = side * RAD * RAD + c * RAD + r
                corners[at, side * STRIP + c * SIDE + r] = 1
                corners[STRIP + at, side * STRIP + c * SIDE + SIDE - RAD + r] = 1
    parts = [np.concatenate([window[0], window[1]], axis=1), axial, strips, strips.T, corners, corners.T]
    return jnp.asarray(np.concatenate([np.pad(t, ((0, 0), (0, 256 - t.shape[1]))) for t in parts]), BF)


class Part:
    def __init__(self, ref, first, rows, lanes):
        self.ref, self.first, self.rows, self.lanes = ref, first, rows, lanes

    def read(self, first=0, rows=None, lane=0, lanes=None):
        start = self.first + first
        end = start + (self.rows - first if rows is None else rows)
        return self.ref[start:end, lane:lane + (self.lanes if lanes is None else lanes)]


def mm(a, b):
    return jnp.dot(a, b, preferred_element_type=F32)


def mm_nt(a, b):
    return lax.dot_general(a, b, (((1,), (1,)), ((), ())), preferred_element_type=F32)


def mm_tn(a, b):
    return lax.dot_general(a, b, (((0,), (0,)), ((), ())), preferred_element_type=F32)


def stacked_heads(block):
    low = lax.broadcasted_iota(jnp.int32, block.shape, 1) < HEAD
    zero = jnp.zeros_like(block)
    return jnp.concatenate([jnp.where(low, block, zero), jnp.where(low, zero, block)], axis=0)


def probabilities(scores, dprob):
    top = jnp.max(scores, axis=0, keepdims=True)
    expo = jnp.exp(scores - top)
    probs = expo * (1.0 / jnp.sum(expo, axis=0, keepdims=True))
    delta = jnp.sum(probs * dprob, axis=0, keepdims=True)
    return probs.astype(BF), (probs * (dprob - delta)).astype(BF)


def kernel(
    nlon, nlat,
    q_hbm, k_hbm, v_hbm, g_hbm, table_hbm, flag_ref, listed_ref,
    out_ref, gq_ref, gk_ref, gv_ref,
    q_ref, k_ref, v_ref, g_ref, table_ref, load_s, flags, columns, bias, xbias, kv, strip_out, corner_out, xkv,
    acc, sides, edge_out, edge_in, side_out, side_in, gx, hop_out, hop_in,
    flag_s, flag_r, strip_s, strip_r, edge_s, edge_r, corner_s, corner_r, ax_s, ax_r,
    bedge_s, bedge_r, bside_s, bside_r, hop_s, hop_r,
):
    loads = [
        pltpu.make_async_copy(src, dst, load_s.at[i])
        for i, (src, dst) in enumerate(
            ((k_hbm, k_ref), (v_hbm, v_ref), (table_hbm, table_ref), (q_hbm, q_ref), (g_hbm, g_ref))
        )
    ]
    for load in loads:
        load.start()
    views = []
    at = 0
    for rows, lanes in ((KEYS, 256), (NSLOT * GROUP, 128), (2 * STRIP, 256), (CELLS, 192), (2 * STRIP, 192), (2 * STRIP, 192)):
        views.append(Part(table_ref, at, rows, lanes))
        at += rows
    near_ref, row_ref, strips_ref, strips_t_ref, corners_ref, corners_t_ref = views
    lon = lax.axis_index("lon")
    lat = lax.axis_index("lat")
    has_up = lat > 0
    has_down = lat < nlat - 1

    def device(dlon, dlat):
        return {"lon": lax.rem(lon + dlon + nlon, nlon), "lat": lax.rem(lat + dlat + nlat, nlat)}

    def remote(src, dst, send, recv, dlon, dlat):
        return pltpu.make_async_remote_copy(
            src_ref=src, dst_ref=dst, send_sem=send, recv_sem=recv,
            device_id=device(dlon, dlat), device_id_type=pl.DeviceIdType.MESH,
        )

    barrier = pltpu.get_barrier_semaphore()
    for dlon, dlat in NEAR:
        pl.semaphore_signal(barrier, inc=1, device_id=device(dlon, dlat), device_id_type=pl.DeviceIdType.MESH)

    flags[RANGE] = flag_ref[...]
    for tile, there in enumerate((has_up, has_down)):
        kv[tile, :, CORNER + TURN:KEYS] = jnp.zeros((2, KEYS - CORNER - TURN, WCH), BF)
        edge_in[tile, :, STRIP + TURN:] = jnp.zeros((2, STRIP - TURN, WCH), BF)

        @pl.when(jnp.logical_not(there))
        def _():
            kv[tile, :, EDGE:CORNER + TURN] = jnp.zeros((2, STRIP + TURN, WCH), BF)
            edge_in[tile, :, 0:STRIP + TURN] = jnp.zeros((2, STRIP + TURN, WCH), BF)

    for part, ref in enumerate((k_ref, v_ref)):
        loads[part].wait()
        for pair in range(XPAIRS):
            at = (2 * pair + part) * PAIR
            xkv[RANGE, :, at:at + PAIR] = ref[:, WCH + pair * PAIR:WCH + (pair + 1) * PAIR]
        kv[0, part, 0:CELLS] = ref[:, :WCH]

    pl.semaphore_wait(barrier, len(NEAR))

    def flag_copy(index):
        dlon, dlat = NEAR[index]
        slot = {0: RANGE, -1: 11, 1: 8}[dlat] - dlon
        return remote(flags.at[RANGE], flags.at[slot], flag_s.at[index], flag_r.at[slot], dlon, dlat)

    def strip_copy(way, piece):
        lanes = pl.ds(piece * WIDE, WIDE)
        return remote(
            strip_out.at[:, pl.ds(way * STRIP, STRIP), lanes], kv.at[0, :, pl.ds(LEFT + way * STRIP, STRIP), lanes],
            strip_s.at[way, piece], strip_r.at[way, piece], 1 - 2 * way, 0,
        )

    def edge_copy(way):
        return remote(
            kv.at[0, :, pl.ds(way * (CELLS - STRIP), STRIP)], kv.at[1 - way, :, pl.ds(EDGE, STRIP)],
            edge_s.at[way], edge_r.at[way], 0, 2 * way - 1,
        )

    def corner_copy(way, piece):
        lanes = pl.ds(pl.multiple_of(piece * WIDE, WIDE), WIDE)
        return remote(
            corner_out.at[:, pl.ds(way * STRIP, TURN), lanes], kv.at[1 - way, :, pl.ds(CORNER, TURN), lanes],
            corner_s.at[way, piece], corner_r.at[way, piece], 0, 2 * way - 1,
        )

    def ax_copy(way, step, pair):
        sign = 1 - 2 * way
        lanes = pl.ds(pair * 2 * PAIR, 2 * PAIR)
        return remote(
            xkv.at[RANGE - sign * step, :, lanes], xkv.at[RANGE - sign * (step + 1), :, lanes],
            ax_s.at[way, step, pair], ax_r.at[way, step, pair], sign, 0,
        )

    def edge_back(way, pair):
        lanes = pl.ds(pl.multiple_of(pair * PAIR, PAIR), PAIR)
        return remote(
            edge_out.at[way, :, pl.ds(0, STRIP + TURN), lanes], edge_in.at[1 - way, :, pl.ds(0, STRIP + TURN), lanes],
            bedge_s.at[way, pair], bedge_r.at[way, pair], 0, 2 * way - 1,
        )

    def side_back(way, pair):
        lanes = pl.ds(pl.multiple_of(pair * PAIR, PAIR), PAIR)
        rows = pl.ds(way * STRIP, STRIP)
        return remote(
            side_out.at[:, rows, lanes], side_in.at[:, rows, lanes],
            bside_s.at[way, pair], bside_r.at[way, pair], 2 * way - 1, 0,
        )

    def hop_back(way, step, pair):
        lanes = pl.ds(pair * 2 * PAIR, 2 * PAIR)
        return remote(
            hop_out.at[way, step, :, lanes], hop_in.at[way, step, :, lanes],
            hop_s.at[way, step, pair], hop_r.at[way, step, pair], 1 - 2 * way, 0,
        )

    def vertical(make, sending):
        @pl.when(has_up)
        def _():
            make(0 if sending else 1)

        @pl.when(has_down)
        def _():
            make(1 if sending else 0)

    def send_strips(piece):
        for way in range(2):
            strip_copy(way, piece).start()

    def turn_strips(piece):
        lanes = slice(piece * WIDE, (piece + 1) * WIDE)
        for way in range(2):
            strip_copy(way, piece).wait_recv()
        for part in range(2):
            strip = kv[0, part, LEFT:EDGE, lanes]
            kv[1, part, LEFT:EDGE, lanes] = strip
            corner_out[part, :, lanes] = mm(corners_ref.read(), strip).astype(BF)
        vertical(lambda way: corner_copy(way, piece).start(), True)

    for pair in range(XPAIRS):
        for way in range(2):
            ax_copy(way, 0, pair).start()
    vertical(lambda way: edge_copy(way).start(), True)
    for index in range(len(NEAR)):
        flag_copy(index).start()
    loads[2].wait()
    for part in range(2):
        strip_out[part] = mm(strips_ref.read(), kv[0, part, 0:CELLS]).astype(BF)
    send_strips(0)
    kv[1, :, 0:CELLS] = kv[0, :, 0:CELLS]

    for index in range(len(NEAR)):
        flag_copy(index).wait_recv()
    for slot in range(13):
        for half in range(2):
            row = jnp.broadcast_to(flags[slot, half:half + 1, :], (128, 128))
            columns[slot, half * 128:(half + 1) * 128] = row.T.astype(BF)

    def sides_of(left, right):
        return jnp.concatenate(
            [mm(strips_ref.read(0, STRIP), columns[left]), mm(strips_ref.read(STRIP), columns[right])], axis=0
        )

    own_flags = columns[RANGE].astype(F32)
    side_flags = sides_of(RANGE - 1, RANGE + 1)
    for tile, there in enumerate((has_up, has_down)):
        base = 7 + 3 * tile
        lives = jnp.where(there, 1.0, 0.0)
        first = CELLS - STRIP if tile == 0 else 0
        edge_flags = columns[base + 1, first:first + STRIP].astype(F32)
        turn = corners_ref.read(STRIP) if tile == 0 else corners_ref.read(0, STRIP)
        corner_flags = mm(turn, sides_of(base, base + 2).astype(BF))
        serves = jnp.concatenate([own_flags, side_flags, edge_flags * lives, corner_flags * lives], axis=0)
        bias[tile] = jnp.where(near_ref.read(lane=tile * 128, lanes=128).astype(F32) + serves > 1.5, 0.0, NEG)
    for group in range(GROUPS):
        serves = jnp.concatenate(
            [
                columns[slot, group * GROUP:(group + 1) * GROUP].astype(F32) * listed_ref[slot:slot + 1, :]
                for slot in range(NSLOT)
            ],
            axis=0,
        )
        xbias[group] = jnp.where(row_ref.read().astype(F32) + serves > 1.5, 0.0, NEG)

    def forward(step):
        for pair in range(XPAIRS):
            for way in range(2):
                ax_copy(way, step - 1, pair).wait_recv()
                ax_copy(way, step, pair).start()

    forward(1)
    for load in loads[3:]:
        load.wait()
    send_strips(1)
    turn_strips(0)
    forward(2)
    send_strips(2)

    def send_sides(pair):
        lanes = pl.ds(pl.multiple_of(pair * PAIR, PAIR), PAIR)
        vertical(lambda way: edge_back(way, pair).wait_recv(), False)
        for part in range(2):
            found = jnp.concatenate(
                [edge_in[0, part, STRIP:2 * STRIP, lanes], edge_in[1, part, STRIP:2 * STRIP, lanes]], axis=0
            )
            side_out[part, :, lanes] = (sides[part, :, lanes] + mm(corners_t_ref.read(), found)).astype(BF)
        for way in range(2):
            side_back(way, pair).start()

    def axial_pair(pair):
        for way in range(2):
            ax_copy(way, 2, pair).wait_recv()
        lanes = slice(WCH + pair * PAIR, WCH + (pair + 1) * PAIR)
        key_lanes = slice(2 * pair * PAIR, (2 * pair + 1) * PAIR)
        value_lanes = slice((2 * pair + 1) * PAIR, (2 * pair + 2) * PAIR)

        def axial_group(group, carry):
            cells = pl.ds(pl.multiple_of(group * GROUP, GROUP), GROUP)
            queries = stacked_heads(q_ref[cells, lanes] * jnp.asarray(SCALE, BF))
            cotangents = stacked_heads(g_ref[cells, lanes])
            keys = xkv[:, cells, key_lanes].reshape(NSLOT * GROUP, PAIR)
            values = xkv[:, cells, value_lanes].reshape(NSLOT * GROUP, PAIR)
            scores = mm_nt(keys, queries) + xbias[group]
            probs, dscore = probabilities(scores, mm_nt(values, cotangents))
            attended = mm_tn(probs, values)
            grad_q = mm_tn(dscore, keys)
            low = lax.broadcasted_iota(jnp.int32, (GROUP, PAIR), 1) < HEAD
            out_ref[cells, lanes] = jnp.where(low, attended[0:GROUP], attended[GROUP:]).astype(BF)
            gq_ref[cells, lanes] = (jnp.where(low, grad_q[0:GROUP], grad_q[GROUP:]) * SCALE).astype(BF)
            gx[:, cells, key_lanes] = mm(dscore, queries).reshape(NSLOT, GROUP, PAIR)
            gx[:, cells, value_lanes] = mm(probs, cotangents).reshape(NSLOT, GROUP, PAIR)
            return carry

        lax.fori_loop(0, GROUPS, axial_group, 0)
        both = slice(2 * pair * PAIR, (2 * pair + 2) * PAIR)
        for way in range(2):
            hop_out[way, 0, :, both] = gx[2 * RANGE * (1 - way), :, both].astype(BF)
            hop_back(way, 0, pair).start()

    def hop(step):
        for pair in range(XPAIRS):
            both = slice(2 * pair * PAIR, (2 * pair + 2) * PAIR)
            for way in range(2):
                slot = 2 * RANGE - step if way == 0 else step
                hop_back(way, step - 1, pair).wait_recv()
                total = gx[slot, :, both] + hop_in[way, step - 1, :, both].astype(F32)
                hop_out[way, step, :, both] = total.astype(BF)
                hop_back(way, step, pair).start()

    def window_pair(pair, carry):
        lanes = pl.ds(pl.multiple_of(pair * PAIR, PAIR), PAIR)

        @pl.when(lax.rem(pair, WIDE // PAIR) == 0)
        def _():
            vertical(lambda way: corner_copy(way, pair // (WIDE // PAIR)).wait_recv(), False)

        grads = []
        for tile in range(2):
            rows = slice(tile * 128, (tile + 1) * 128)
            queries = stacked_heads(q_ref[rows, lanes] * jnp.asarray(SCALE, BF))
            cotangents = stacked_heads(g_ref[rows, lanes])
            keys = kv[tile, 0, :, lanes]
            values = kv[tile, 1, :, lanes]
            penalty = bias[tile]
            scores = mm_nt(keys, queries) + jnp.concatenate([penalty, penalty], axis=1)
            probs, dscore = probabilities(scores, mm_nt(values, cotangents))
            attended = mm_tn(values, probs)
            grad_q = mm_tn(keys, dscore)
            for result, ref, factor in ((attended, out_ref, 1.0), (grad_q, gq_ref, SCALE)):
                both = jnp.concatenate([result[0:HEAD, 0:128], result[HEAD:, 128:]], axis=0)
                ref[rows, lanes] = (both.T * factor).astype(BF)
            grads.append((mm(dscore, queries), mm(probs, cotangents)))
        for part in range(2):
            first, second = grads[0][part], grads[1][part]
            acc[part, :, lanes] = first[0:CELLS] + second[0:CELLS]
            sides[part, :, lanes] = first[LEFT:EDGE] + second[LEFT:EDGE]
            edge_out[0, part, :, lanes] = first[EDGE:].astype(BF)
            edge_out[1, part, :, lanes] = second[EDGE:].astype(BF)
        vertical(lambda way: edge_back(way, pair).start(), True)

        for step in range(1, RANGE):
            @pl.when(pair == 2 * step - 1)
            def _():
                hop(step)

        @pl.when(pair >= LAG)
        def _():
            send_sides(pair - LAG)

        return carry

    for pair in range(XPAIRS):
        axial_pair(pair)
        turn_strips(1 + pair)
    vertical(lambda way: edge_copy(way).wait_recv(), False)
    lax.fori_loop(0, PAIRS, window_pair, 0)
    for late in range(LAG):
        send_sides(PAIRS - LAG + late)

    for pair in range(XPAIRS):
        lanes = slice(WCH + pair * PAIR, WCH + (pair + 1) * PAIR)
        for way in range(2):
            hop_back(way, RANGE - 1, pair).wait_recv()
        for part, ref in enumerate((gk_ref, gv_ref)):
            at = slice((2 * pair + part) * PAIR, (2 * pair + part + 1) * PAIR)
            total = gx[RANGE, :, at]
            for way in range(2):
                total = total + hop_in[way, RANGE - 1, :, at].astype(F32)
            ref[:, lanes] = total.astype(BF)

    for piece in range(PIECES):
        lanes = slice(piece * WIDE, (piece + 1) * WIDE)
        for pair in range(piece * (WIDE // PAIR), (piece + 1) * (WIDE // PAIR)):
            for way in range(2):
                side_back(way, pair).wait_recv()
        for part, ref in enumerate((gk_ref, gv_ref)):
            total = acc[part, :, lanes] + mm(strips_t_ref.read(), side_in[part, :, lanes])
            top = total[0:STRIP] + edge_in[0, part, 0:STRIP, lanes].astype(F32)
            bottom = total[CELLS - STRIP:] + edge_in[1, part, 0:STRIP, lanes].astype(F32)
            ref[0:STRIP, lanes] = top.astype(BF)
            ref[STRIP:CELLS - STRIP, lanes] = total[STRIP:CELLS - STRIP].astype(BF)
            ref[CELLS - STRIP:, lanes] = bottom.astype(BF)

    for index in range(len(NEAR)):
        flag_copy(index).wait_send()
    for way in range(2):
        for piece in range(PIECES):
            strip_copy(way, piece).wait_send()
        for step in range(RANGE):
            for pair in range(XPAIRS):
                ax_copy(way, step, pair).wait_send()
                hop_back(way, step, pair).wait_send()
        for pair in range(PAIRS):
            side_back(way, pair).wait_send()
    vertical(lambda way: edge_copy(way).wait_send(), True)
    for piece in range(PIECES):
        vertical(lambda way: corner_copy(way, piece).wait_send(), True)
    for pair in range(PAIRS):
        vertical(lambda way: edge_back(way, pair).wait_send(), True)


def per_device(nlon, nlat, queries, key_vectors, value_vectors, grad_out, key_mask, block_lists):
    shape = queries.shape
    flat = [x.reshape(CELLS, shape[-1]) for x in (queries, key_vectors, value_vectors, grad_out)]
    flag = jnp.pad((key_mask > 0).astype(F32).reshape(2, 128), ((0, 6), (0, 0)))
    offset = (block_lists[0] - lax.axis_index("lon") + RANGE + nlon) % nlon
    listed = jnp.any(jnp.arange(8)[:, None] == offset[None, :], axis=1)
    listed = jnp.broadcast_to(listed[:, None], (8, 128)).astype(F32)
    table = tables()
    vmem = pl.BlockSpec(memory_space=pltpu.VMEM)
    dma = lambda *s: pltpu.SemaphoreType.DMA(s)
    outs = pl.pallas_call(
        functools.partial(kernel, nlon, nlat),
        out_shape=[jax.ShapeDtypeStruct((CELLS, shape[-1]), BF)] * 4,
        in_specs=[pl.BlockSpec(memory_space=pltpu.HBM)] * 5 + [vmem] * 2,
        out_specs=[vmem] * 4,
        scratch_shapes=[
            *[pltpu.VMEM((CELLS, shape[-1]), BF)] * 4,
            pltpu.VMEM(table.shape, BF),
            dma(5),
            pltpu.VMEM((13, 8, 128), F32),
            pltpu.VMEM((13, CELLS, 128), BF),
            pltpu.VMEM((2, KEYS, 128), F32),
            pltpu.VMEM((GROUPS, NSLOT * GROUP, 128), F32),
            pltpu.VMEM((2, 2, KEYS, WCH), BF),
            pltpu.VMEM((2, 2 * STRIP, WCH), BF),
            pltpu.VMEM((2, 2 * STRIP, WCH), BF),
            pltpu.VMEM((NSLOT, CELLS, 2 * XPAIRS * PAIR), BF),
            pltpu.VMEM((2, CELLS, WCH), F32),
            pltpu.VMEM((2, 2 * STRIP, WCH), F32),
            pltpu.VMEM((2, 2, 2 * STRIP, WCH), BF),
            pltpu.VMEM((2, 2, 2 * STRIP, WCH), BF),
            pltpu.VMEM((2, 2 * STRIP, WCH), BF),
            pltpu.VMEM((2, 2 * STRIP, WCH), BF),
            pltpu.VMEM((NSLOT, CELLS, 2 * XPAIRS * PAIR), F32),
            pltpu.VMEM((2, RANGE, CELLS, 2 * XPAIRS * PAIR), BF),
            pltpu.VMEM((2, RANGE, CELLS, 2 * XPAIRS * PAIR), BF),
            dma(len(NEAR)), dma(13), dma(2, PIECES), dma(2, PIECES), dma(2), dma(2), dma(2, PIECES), dma(2, PIECES),
            dma(2, RANGE, XPAIRS), dma(2, RANGE, XPAIRS), dma(2, PAIRS), dma(2, PAIRS), dma(2, PAIRS), dma(2, PAIRS),
            dma(2, RANGE, XPAIRS), dma(2, RANGE, XPAIRS),
        ],
        compiler_params=pltpu.CompilerParams(
            collective_id=0, has_side_effects=True, vmem_limit_bytes=52 * 1024 * 1024
        ),
        cost_estimate=pl.CostEstimate(flops=4_000_000_000, bytes_accessed=5_000_000, transcendentals=3_000_000),
    )(*flat, table, flag, listed)
    return tuple(x.reshape(shape) for x in outs)


def solution(mesh):
    cells = P("lat", "lon", None)
    return jax.shard_map(
        functools.partial(per_device, mesh.shape["lon"], mesh.shape["lat"]),
        mesh=mesh,
        in_specs=(cells, cells, cells, cells, P("lat", "lon"), P("lon", None)),
        out_specs=(cells, cells, cells, cells),
        check_vma=False,
    )
```

```python
import functools

import jax
import jax.numpy as jnp
import numpy as np
from jax import lax
from jax.experimental import pallas as pl
from jax.experimental.pallas import tpu as pltpu
from jax.sharding import PartitionSpec as P

HEAD = 64
NB_HEADS = 12
RAD = 6
RANGE = 3
SIDE = 16
CELLS = SIDE * SIDE
WCH = NB_HEADS * HEAD
PAIR = 2 * HEAD
PAIRS = WCH // PAIR
XPAIRS = 2
STRIP = RAD * SIDE
LEFT = CELLS
RIGHT = CELLS + STRIP
EDGE = CELLS + 2 * STRIP
CORNER = EDGE + STRIP
KEYS = CORNER + STRIP
NSLOT = 2 * RANGE + 1
GROUP = 64
TURN = 80
LAG = 2
PIECES = 3
WIDE = WCH // PIECES
GROUPS = CELLS // GROUP
NEG = -1e30
SCALE = HEAD**-0.5
BF = jnp.bfloat16
F32 = jnp.float32
NEAR = [(o, 0) for o in (1, -1, 2, -2, 3, -3)] + [(o, a) for a in (-1, 1) for o in (0, 1, -1)]


def key_places(tile):
    rows = np.full(KEYS, 1000)
    cols = np.full(KEYS, 1000)
    own = np.arange(CELLS)
    rows[:CELLS], cols[:CELLS] = own // SIDE, own % SIDE
    strip = np.arange(STRIP)
    rows[LEFT:RIGHT], cols[LEFT:RIGHT] = strip % SIDE, strip // SIDE - RAD
    rows[RIGHT:EDGE], cols[RIGHT:EDGE] = strip % SIDE, strip // SIDE + SIDE
    first = -RAD if tile == 0 else SIDE
    rows[EDGE:CORNER], cols[EDGE:CORNER] = first + strip // SIDE, strip % SIDE
    for side in range(2):
        for c in range(RAD):
            for r in range(RAD):
                at = CORNER + side * RAD * RAD + c * RAD + r
                rows[at] = first + r
                cols[at] = c - RAD if side == 0 else c + SIDE
    return rows, cols


def tables():
    window = np.zeros((2, KEYS, 128), np.float32)
    lane = np.arange(128)
    for tile in range(2):
        rows, cols = key_places(tile)
        q_row, q_col = lane // SIDE + 8 * tile, lane % SIDE
        dr = rows[:, None] - q_row[None, :]
        dc = cols[:, None] - q_col[None, :]
        window[tile] = ((np.abs(dr) <= RAD) & (np.abs(dc) <= RAD)) + 1.0 * ((dr == 0) & (dc == 0))
    slot = np.arange(NSLOT * GROUP)
    cell = slot % GROUP
    query = lane % GROUP
    axial = (cell[:, None] // SIDE == query[None, :] // SIDE) + 1.0 * (
        (cell[:, None] == query[None, :]) & (slot[:, None] // GROUP == RANGE)
    )
    strips = np.zeros((2 * STRIP, CELLS), np.float32)
    for c in range(RAD):
        for r in range(SIDE):
            strips[c * SIDE + r, r * SIDE + SIDE - RAD + c] = 1
            strips[STRIP + c * SIDE + r, r * SIDE + c] = 1
    corners = np.zeros((2 * STRIP, 2 * STRIP), np.float32)
    for side in range(2):
        for c in range(RAD):
            for r in range(RAD):
                at = side * RAD * RAD + c * RAD + r
                corners[at, side * STRIP + c * SIDE + r] = 1
                corners[STRIP + at, side * STRIP + c * SIDE + SIDE - RAD + r] = 1
    parts = [np.concatenate([window[0], window[1]], axis=1), axial, strips, strips.T, corners, corners.T]
    return jnp.asarray(np.concatenate([np.pad(t, ((0, 0), (0, 256 - t.shape[1]))) for t in parts]), BF)


class Part:
    def __init__(self, ref, first, rows, lanes):
        self.ref, self.first, self.rows, self.lanes = ref, first, rows, lanes

    def read(self, first=0, rows=None, lane=0, lanes=None):
        start = self.first + first
        end = start + (self.rows - first if rows is None else rows)
        return self.ref[start:end, lane:lane + (self.lanes if lanes is None else lanes)]


def mm(a, b):
    return jnp.dot(a, b, preferred_element_type=F32)


def mm_nt(a, b):
    return lax.dot_general(a, b, (((1,), (1,)), ((), ())), preferred_element_type=F32)


def mm_tn(a, b):
    return lax.dot_general(a, b, (((0,), (0,)), ((), ())), preferred_element_type=F32)


def stacked_heads(block):
    low = lax.broadcasted_iota(jnp.int32, block.shape, 1) < HEAD
    zero = jnp.zeros_like(block)
    return jnp.concatenate([jnp.where(low, block, zero), jnp.where(low, zero, block)], axis=0)


def probabilities(scores, dprob):
    top = jnp.max(scores, axis=0, keepdims=True)
    expo = jnp.exp(scores - top)
    probs = expo * (1.0 / jnp.sum(expo, axis=0, keepdims=True))
    delta = jnp.sum(probs * dprob, axis=0, keepdims=True)
    return probs.astype(BF), (probs * (dprob - delta)).astype(BF)


def kernel(
    nlon, nlat,
    q_hbm, k_hbm, v_hbm, g_hbm, table_hbm, flag_ref, listed_ref,
    out_ref, gq_ref, gk_ref, gv_ref,
    q_ref, k_ref, v_ref, g_ref, table_ref, load_s, flags, columns, bias, xbias, kv, strip_out, corner_out, xkv,
    acc, sides, edge_out, edge_in, side_out, side_in, gx, hop_out, hop_in,
    flag_s, flag_r, strip_s, strip_r, edge_s, edge_r, corner_s, corner_r, ax_s, ax_r,
    bedge_s, bedge_r, bside_s, bside_r, hop_s, hop_r,
):
    loads = [
        pltpu.make_async_copy(src, dst, load_s.at[i])
        for i, (src, dst) in enumerate(
            ((k_hbm, k_ref), (v_hbm, v_ref), (table_hbm, table_ref), (q_hbm, q_ref), (g_hbm, g_ref))
        )
    ]
    for load in loads:
        load.start()
    views = []
    at = 0
    for rows, lanes in ((KEYS, 256), (NSLOT * GROUP, 128), (2 * STRIP, 256), (CELLS, 192), (2 * STRIP, 192), (2 * STRIP, 192)):
        views.append(Part(table_ref, at, rows, lanes))
        at += rows
    near_ref, row_ref, strips_ref, strips_t_ref, corners_ref, corners_t_ref = views
    lon = lax.axis_index("lon")
    lat = lax.axis_index("lat")
    has_up = lat > 0
    has_down = lat < nlat - 1

    def device(dlon, dlat):
        return {"lon": lax.rem(lon + dlon + nlon, nlon), "lat": lax.rem(lat + dlat + nlat, nlat)}

    def remote(src, dst, send, recv, dlon, dlat):
        return pltpu.make_async_remote_copy(
            src_ref=src, dst_ref=dst, send_sem=send, recv_sem=recv,
            device_id=device(dlon, dlat), device_id_type=pl.DeviceIdType.MESH,
        )

    barrier = pltpu.get_barrier_semaphore()
    for dlon, dlat in NEAR:
        pl.semaphore_signal(barrier, inc=1, device_id=device(dlon, dlat), device_id_type=pl.DeviceIdType.MESH)

    flags[RANGE] = flag_ref[...]
    for tile, there in enumerate((has_up, has_down)):
        kv[tile, :, CORNER + TURN:KEYS] = jnp.zeros((2, KEYS - CORNER - TURN, WCH), BF)
        edge_in[tile, :, STRIP + TURN:] = jnp.zeros((2, STRIP - TURN, WCH), BF)

        @pl.when(jnp.logical_not(there))
        def _():
            kv[tile, :, EDGE:CORNER + TURN] = jnp.zeros((2, STRIP + TURN, WCH), BF)
            edge_in[tile, :, 0:STRIP + TURN] = jnp.zeros((2, STRIP + TURN, WCH), BF)

    for part, ref in enumerate((k_ref, v_ref)):
        loads[part].wait()
        for pair in range(XPAIRS):
            at = (2 * pair + part) * PAIR
            xkv[RANGE, :, at:at + PAIR] = ref[:, WCH + pair * PAIR:WCH + (pair + 1) * PAIR]
        kv[0, part, 0:CELLS] = ref[:, :WCH]

    pl.semaphore_wait(barrier, len(NEAR))

    def flag_copy(index):
        dlon, dlat = NEAR[index]
        slot = {0: RANGE, -1: 11, 1: 8}[dlat] - dlon
        return remote(flags.at[RANGE], flags.at[slot], flag_s.at[index], flag_r.at[slot], dlon, dlat)

    def strip_copy(way, piece):
        lanes = pl.ds(piece * WIDE, WIDE)
        return remote(
            strip_out.at[:, pl.ds(way * STRIP, STRIP), lanes], kv.at[0, :, pl.ds(LEFT + way * STRIP, STRIP), lanes],
            strip_s.at[way, piece], strip_r.at[way, piece], 1 - 2 * way, 0,
        )

    def edge_copy(way):
        return remote(
            kv.at[0, :, pl.ds(way * (CELLS - STRIP), STRIP)], kv.at[1 - way, :, pl.ds(EDGE, STRIP)],
            edge_s.at[way], edge_r.at[way], 0, 2 * way - 1,
        )

    def corner_copy(way, piece):
        lanes = pl.ds(pl.multiple_of(piece * WIDE, WIDE), WIDE)
        return remote(
            corner_out.at[:, pl.ds(way * STRIP, TURN), lanes], kv.at[1 - way, :, pl.ds(CORNER, TURN), lanes],
            corner_s.at[way, piece], corner_r.at[way, piece], 0, 2 * way - 1,
        )

    def ax_copy(way, step, pair):
        sign = 1 - 2 * way
        lanes = pl.ds(pair * 2 * PAIR, 2 * PAIR)
        return remote(
            xkv.at[RANGE - sign * step, :, lanes], xkv.at[RANGE - sign * (step + 1), :, lanes],
            ax_s.at[way, step, pair], ax_r.at[way, step, pair], sign, 0,
        )

    def edge_back(way, pair):
        lanes = pl.ds(pl.multiple_of(pair * PAIR, PAIR), PAIR)
        return remote(
            edge_out.at[way, :, pl.ds(0, STRIP + TURN), lanes], edge_in.at[1 - way, :, pl.ds(0, STRIP + TURN), lanes],
            bedge_s.at[way, pair], bedge_r.at[way, pair], 0, 2 * way - 1,
        )

    def side_back(way, pair):
        lanes = pl.ds(pl.multiple_of(pair * PAIR, PAIR), PAIR)
        rows = pl.ds(way * STRIP, STRIP)
        return remote(
            side_out.at[:, rows, lanes], side_in.at[:, rows, lanes],
            bside_s.at[way, pair], bside_r.at[way, pair], 2 * way - 1, 0,
        )

    def hop_back(way, step, pair):
        lanes = pl.ds(pair * 2 * PAIR, 2 * PAIR)
        return remote(
            hop_out.at[way, step, :, lanes], hop_in.at[way, step, :, lanes],
            hop_s.at[way, step, pair], hop_r.at[way, step, pair], 1 - 2 * way, 0,
        )

    def vertical(make, sending):
        @pl.when(has_up)
        def _():
            make(0 if sending else 1)

        @pl.when(has_down)
        def _():
            make(1 if sending else 0)

    def send_strips(piece):
        for way in range(2):
            strip_copy(way, piece).start()

    def turn_strips(piece):
        lanes = slice(piece * WIDE, (piece + 1) * WIDE)
        for way in range(2):
            strip_copy(way, piece).wait_recv()
        for part in range(2):
            strip = kv[0, part, LEFT:EDGE, lanes]
            kv[1, part, LEFT:EDGE, lanes] = strip
            corner_out[part, :, lanes] = mm(corners_ref.read(), strip).astype(BF)
        vertical(lambda way: corner_copy(way, piece).start(), True)

    for pair in range(XPAIRS):
        for way in range(2):
            ax_copy(way, 0, pair).start()
    vertical(lambda way: edge_copy(way).start(), True)
    for index in range(len(NEAR)):
        flag_copy(index).start()
    loads[2].wait()
    for part in range(2):
        strip_out[part] = mm(strips_ref.read(), kv[0, part, 0:CELLS]).astype(BF)
    send_strips(0)
    kv[1, :, 0:CELLS] = kv[0, :, 0:CELLS]

    for index in range(len(NEAR)):
        flag_copy(index).wait_recv()
    for slot in range(13):
        for half in range(2):
            row = jnp.broadcast_to(flags[slot, half:half + 1, :], (128, 128))
            columns[slot, half * 128:(half + 1) * 128] = row.T.astype(BF)

    def sides_of(left, right):
        return jnp.concatenate(
            [mm(strips_ref.read(0, STRIP), columns[left]), mm(strips_ref.read(STRIP), columns[right])], axis=0
        )

    own_flags = columns[RANGE].astype(F32)
    side_flags = sides_of(RANGE - 1, RANGE + 1)
    for tile, there in enumerate((has_up, has_down)):
        base = 7 + 3 * tile
        lives = jnp.where(there, 1.0, 0.0)
        first = CELLS - STRIP if tile == 0 else 0
        edge_flags = columns[base + 1, first:first + STRIP].astype(F32)
        turn = corners_ref.read(STRIP) if tile == 0 else corners_ref.read(0, STRIP)
        corner_flags = mm(turn, sides_of(base, base + 2).astype(BF))
        serves = jnp.concatenate([own_flags, side_flags, edge_flags * lives, corner_flags * lives], axis=0)
        bias[tile] = jnp.where(near_ref.read(lane=tile * 128, lanes=128).astype(F32) + serves > 1.5, 0.0, NEG)
    for group in range(GROUPS):
        serves = jnp.concatenate(
            [
                columns[slot, group * GROUP:(group + 1) * GROUP].astype(F32) * listed_ref[slot:slot + 1, :]
                for slot in range(NSLOT)
            ],
            axis=0,
        )
        xbias[group] = jnp.where(row_ref.read().astype(F32) + serves > 1.5, 0.0, NEG)

    def forward(step):
        for pair in range(XPAIRS):
            for way in range(2):
                ax_copy(way, step - 1, pair).wait_recv()
                ax_copy(way, step, pair).start()

    forward(1)
    for load in loads[3:]:
        load.wait()
    send_strips(1)
    turn_strips(0)
    forward(2)
    send_strips(2)

    def send_sides(pair):
        lanes = pl.ds(pl.multiple_of(pair * PAIR, PAIR), PAIR)
        vertical(lambda way: edge_back(way, pair).wait_recv(), False)
        for part in range(2):
            found = jnp.concatenate(
                [edge_in[0, part, STRIP:2 * STRIP, lanes], edge_in[1, part, STRIP:2 * STRIP, lanes]], axis=0
            )
            side_out[part, :, lanes] = (sides[part, :, lanes] + mm(corners_t_ref.read(), found)).astype(BF)
        for way in range(2):
            side_back(way, pair).start()

    def axial_pair(pair):
        for way in range(2):
            ax_copy(way, 2, pair).wait_recv()
        lanes = slice(WCH + pair * PAIR, WCH + (pair + 1) * PAIR)
        key_lanes = slice(2 * pair * PAIR, (2 * pair + 1) * PAIR)
        value_lanes = slice((2 * pair + 1) * PAIR, (2 * pair + 2) * PAIR)

        def axial_group(group, carry):
            cells = pl.ds(pl.multiple_of(group * GROUP, GROUP), GROUP)
            queries = stacked_heads(q_ref[cells, lanes] * jnp.asarray(SCALE, BF))
            cotangents = stacked_heads(g_ref[cells, lanes])
            keys = xkv[:, cells, key_lanes].reshape(NSLOT * GROUP, PAIR)
            values = xkv[:, cells, value_lanes].reshape(NSLOT * GROUP, PAIR)
            scores = mm_nt(keys, queries) + xbias[group]
            probs, dscore = probabilities(scores, mm_nt(values, cotangents))
            attended = mm_tn(probs, values)
            grad_q = mm_tn(dscore, keys)
            low = lax.broadcasted_iota(jnp.int32, (GROUP, PAIR), 1) < HEAD
            out_ref[cells, lanes] = jnp.where(low, attended[0:GROUP], attended[GROUP:]).astype(BF)
            gq_ref[cells, lanes] = (jnp.where(low, grad_q[0:GROUP], grad_q[GROUP:]) * SCALE).astype(BF)
            gx[:, cells, key_lanes] = mm(dscore, queries).reshape(NSLOT, GROUP, PAIR)
            gx[:, cells, value_lanes] = mm(probs, cotangents).reshape(NSLOT, GROUP, PAIR)
            return carry

        lax.fori_loop(0, GROUPS, axial_group, 0)
        both = slice(2 * pair * PAIR, (2 * pair + 2) * PAIR)
        for way in range(2):
            hop_out[way, 0, :, both] = gx[2 * RANGE * (1 - way), :, both].astype(BF)
            hop_back(way, 0, pair).start()

    def hop(step):
        for pair in range(XPAIRS):
            both = slice(2 * pair * PAIR, (2 * pair + 2) * PAIR)
            for way in range(2):
                slot = 2 * RANGE - step if way == 0 else step
                hop_back(way, step - 1, pair).wait_recv()
                total = gx[slot, :, both] + hop_in[way, step - 1, :, both].astype(F32)
                hop_out[way, step, :, both] = total.astype(BF)
                hop_back(way, step, pair).start()

    def window_pair(pair, carry):
        lanes = pl.ds(pl.multiple_of(pair * PAIR, PAIR), PAIR)

        @pl.when(lax.rem(pair, WIDE // PAIR) == 0)
        def _():
            vertical(lambda way: corner_copy(way, pair // (WIDE // PAIR)).wait_recv(), False)

        grads = []
        for tile in range(2):
            rows = slice(tile * 128, (tile + 1) * 128)
            queries = stacked_heads(q_ref[rows, lanes] * jnp.asarray(SCALE, BF))
            cotangents = stacked_heads(g_ref[rows, lanes])
            keys = kv[tile, 0, :, lanes]
            values = kv[tile, 1, :, lanes]
            penalty = bias[tile]
            scores = mm_nt(keys, queries) + jnp.concatenate([penalty, penalty], axis=1)
            probs, dscore = probabilities(scores, mm_nt(values, cotangents))
            attended = mm_tn(values, probs)
            grad_q = mm_tn(keys, dscore)
            for result, ref, factor in ((attended, out_ref, 1.0), (grad_q, gq_ref, SCALE)):
                both = jnp.concatenate([result[0:HEAD, 0:128], result[HEAD:, 128:]], axis=0)
                ref[rows, lanes] = (both.T * factor).astype(BF)
            grads.append((mm(dscore, queries), mm(probs, cotangents)))
        for part in range(2):
            first, second = grads[0][part], grads[1][part]
            acc[part, :, lanes] = first[0:CELLS] + second[0:CELLS]
            sides[part, :, lanes] = first[LEFT:EDGE] + second[LEFT:EDGE]
            edge_out[0, part, :, lanes] = first[EDGE:].astype(BF)
            edge_out[1, part, :, lanes] = second[EDGE:].astype(BF)
        vertical(lambda way: edge_back(way, pair).start(), True)

        for step in range(1, RANGE):
            @pl.when(pair == 2 * step)
            def _():
                hop(step)

        @pl.when(pair >= LAG)
        def _():
            send_sides(pair - LAG)

        return carry

    for pair in range(XPAIRS):
        axial_pair(pair)
        turn_strips(1 + pair)
    vertical(lambda way: edge_copy(way).wait_recv(), False)
    lax.fori_loop(0, PAIRS, window_pair, 0)
    for late in range(LAG):
        send_sides(PAIRS - LAG + late)

    for pair in range(XPAIRS):
        lanes = slice(WCH + pair * PAIR, WCH + (pair + 1) * PAIR)
        for way in range(2):
            hop_back(way, RANGE - 1, pair).wait_recv()
        for part, ref in enumerate((gk_ref, gv_ref)):
            at = slice((2 * pair + part) * PAIR, (2 * pair + part + 1) * PAIR)
            total = gx[RANGE, :, at]
            for way in range(2):
                total = total + hop_in[way, RANGE - 1, :, at].astype(F32)
            ref[:, lanes] = total.astype(BF)

    for piece in range(PIECES):
        lanes = slice(piece * WIDE, (piece + 1) * WIDE)
        for pair in range(piece * (WIDE // PAIR), (piece + 1) * (WIDE // PAIR)):
            for way in range(2):
                side_back(way, pair).wait_recv()
        for part, ref in enumerate((gk_ref, gv_ref)):
            total = acc[part, :, lanes] + mm(strips_t_ref.read(), side_in[part, :, lanes])
            top = total[0:STRIP] + edge_in[0, part, 0:STRIP, lanes].astype(F32)
            bottom = total[CELLS - STRIP:] + edge_in[1, part, 0:STRIP, lanes].astype(F32)
            ref[0:STRIP, lanes] = top.astype(BF)
            ref[STRIP:CELLS - STRIP, lanes] = total[STRIP:CELLS - STRIP].astype(BF)
            ref[CELLS - STRIP:, lanes] = bottom.astype(BF)

    for index in range(len(NEAR)):
        flag_copy(index).wait_send()
    for way in range(2):
        for piece in range(PIECES):
            strip_copy(way, piece).wait_send()
        for step in range(RANGE):
            for pair in range(XPAIRS):
                ax_copy(way, step, pair).wait_send()
                hop_back(way, step, pair).wait_send()
        for pair in range(PAIRS):
            side_back(way, pair).wait_send()
    vertical(lambda way: edge_copy(way).wait_send(), True)
    for piece in range(PIECES):
        vertical(lambda way: corner_copy(way, piece).wait_send(), True)
    for pair in range(PAIRS):
        vertical(lambda way: edge_back(way, pair).wait_send(), True)


def store_kernel(*refs):
    count = len(refs) // 2
    sources, targets, done = refs[:count], refs[count:2 * count], refs[-1]
    copies = [
        pltpu.make_async_copy(src, dst, done.at[i]) for i, (src, dst) in enumerate(zip(sources, targets))
    ]
    for copy in copies:
        copy.start()
    for copy in copies:
        copy.wait()


def per_device(nlon, nlat, queries, key_vectors, value_vectors, grad_out, key_mask, block_lists):
    shape = queries.shape
    flat = [x.reshape(CELLS, shape[-1]) for x in (queries, key_vectors, value_vectors, grad_out)]
    flag = jnp.pad((key_mask > 0).astype(F32).reshape(2, 128), ((0, 6), (0, 0)))
    offset = (block_lists[0] - lax.axis_index("lon") + RANGE + nlon) % nlon
    listed = jnp.any(jnp.arange(8)[:, None] == offset[None, :], axis=1)
    listed = jnp.broadcast_to(listed[:, None], (8, 128)).astype(F32)
    table = tables()
    vmem = pl.BlockSpec(memory_space=pltpu.VMEM)
    dma = lambda *s: pltpu.SemaphoreType.DMA(s)
    outs = pl.pallas_call(
        functools.partial(kernel, nlon, nlat),
        out_shape=[jax.ShapeDtypeStruct((CELLS, shape[-1]), BF)] * 4,
        in_specs=[pl.BlockSpec(memory_space=pltpu.HBM)] * 5 + [vmem] * 2,
        out_specs=[vmem] * 4,
        scratch_shapes=[
            *[pltpu.VMEM((CELLS, shape[-1]), BF)] * 4,
            pltpu.VMEM(table.shape, BF),
            dma(5),
            pltpu.VMEM((13, 8, 128), F32),
            pltpu.VMEM((13, CELLS, 128), BF),
            pltpu.VMEM((2, KEYS, 128), F32),
            pltpu.VMEM((GROUPS, NSLOT * GROUP, 128), F32),
            pltpu.VMEM((2, 2, KEYS, WCH), BF),
            pltpu.VMEM((2, 2 * STRIP, WCH), BF),
            pltpu.VMEM((2, 2 * STRIP, WCH), BF),
            pltpu.VMEM((NSLOT, CELLS, 2 * XPAIRS * PAIR), BF),
            pltpu.VMEM((2, CELLS, WCH), F32),
            pltpu.VMEM((2, 2 * STRIP, WCH), F32),
            pltpu.VMEM((2, 2, 2 * STRIP, WCH), BF),
            pltpu.VMEM((2, 2, 2 * STRIP, WCH), BF),
            pltpu.VMEM((2, 2 * STRIP, WCH), BF),
            pltpu.VMEM((2, 2 * STRIP, WCH), BF),
            pltpu.VMEM((NSLOT, CELLS, 2 * XPAIRS * PAIR), F32),
            pltpu.VMEM((2, RANGE, CELLS, 2 * XPAIRS * PAIR), BF),
            pltpu.VMEM((2, RANGE, CELLS, 2 * XPAIRS * PAIR), BF),
            dma(len(NEAR)), dma(13), dma(2, PIECES), dma(2, PIECES), dma(2), dma(2), dma(2, PIECES), dma(2, PIECES),
            dma(2, RANGE, XPAIRS), dma(2, RANGE, XPAIRS), dma(2, PAIRS), dma(2, PAIRS), dma(2, PAIRS), dma(2, PAIRS),
            dma(2, RANGE, XPAIRS), dma(2, RANGE, XPAIRS),
        ],
        compiler_params=pltpu.CompilerParams(
            collective_id=0, has_side_effects=True, vmem_limit_bytes=52 * 1024 * 1024
        ),
        cost_estimate=pl.CostEstimate(flops=4_000_000_000, bytes_accessed=5_000_000, transcendentals=3_000_000),
    )(*flat, table, flag, listed)
    stored = pl.pallas_call(
        store_kernel,
        out_shape=[jax.ShapeDtypeStruct((CELLS, shape[-1]), BF)] * 4,
        in_specs=[pl.BlockSpec(memory_space=pl.ANY)] * 4,
        out_specs=[pl.BlockSpec(memory_space=pltpu.HBM)] * 4,
        scratch_shapes=[dma(4)],
        compiler_params=pltpu.CompilerParams(vmem_limit_bytes=1024 * 1024),
        cost_estimate=pl.CostEstimate(flops=0, bytes_accessed=4_000_000, transcendentals=0),
    )(*outs)
    return tuple(x.reshape(shape) for x in stored)


def solution(mesh):
    cells = P("lat", "lon", None)
    return jax.shard_map(
        functools.partial(per_device, mesh.shape["lon"], mesh.shape["lat"]),
        mesh=mesh,
        in_specs=(cells, cells, cells, cells, P("lat", "lon"), P("lon", None)),
        out_specs=(cells, cells, cells, cells),
        check_vma=False,
    )
```

```python
import functools

import jax
import jax.numpy as jnp
import numpy as np
from jax import lax
from jax.experimental import pallas as pl
from jax.experimental.pallas import tpu as pltpu
from jax.sharding import PartitionSpec as P

HEAD = 64
NB_HEADS = 12
RAD = 6
RANGE = 3
SIDE = 16
CELLS = SIDE * SIDE
WCH = NB_HEADS * HEAD
PAIR = 2 * HEAD
PAIRS = WCH // PAIR
XPAIRS = 2
STRIP = RAD * SIDE
LEFT = CELLS
RIGHT = CELLS + STRIP
EDGE = CELLS + 2 * STRIP
CORNER = EDGE + STRIP
KEYS = CORNER + STRIP
NSLOT = 2 * RANGE + 1
GROUP = 64
TURN = 80
LAG = 2
PIECES = 3
WIDE = WCH // PIECES
GROUPS = CELLS // GROUP
NEG = -1e30
SCALE = HEAD**-0.5
BF = jnp.bfloat16
F32 = jnp.float32
NEAR = [(o, 0) for o in (1, -1, 2, -2, 3, -3)] + [(o, a) for a in (-1, 1) for o in (0, 1, -1)]


def key_places(tile):
    rows = np.full(KEYS, 1000)
    cols = np.full(KEYS, 1000)
    own = np.arange(CELLS)
    rows[:CELLS], cols[:CELLS] = own // SIDE, own % SIDE
    strip = np.arange(STRIP)
    rows[LEFT:RIGHT], cols[LEFT:RIGHT] = strip % SIDE, strip // SIDE - RAD
    rows[RIGHT:EDGE], cols[RIGHT:EDGE] = strip % SIDE, strip // SIDE + SIDE
    first = -RAD if tile == 0 else SIDE
    rows[EDGE:CORNER], cols[EDGE:CORNER] = first + strip // SIDE, strip % SIDE
    for side in range(2):
        for c in range(RAD):
            for r in range(RAD):
                at = CORNER + side * RAD * RAD + c * RAD + r
                rows[at] = first + r
                cols[at] = c - RAD if side == 0 else c + SIDE
    return rows, cols


def tables():
    window = np.zeros((2, KEYS, 128), np.float32)
    lane = np.arange(128)
    for tile in range(2):
        rows, cols = key_places(tile)
        q_row, q_col = lane // SIDE + 8 * tile, lane % SIDE
        dr = rows[:, None] - q_row[None, :]
        dc = cols[:, None] - q_col[None, :]
        window[tile] = ((np.abs(dr) <= RAD) & (np.abs(dc) <= RAD)) + 1.0 * ((dr == 0) & (dc == 0))
    slot = np.arange(NSLOT * GROUP)
    cell = slot % GROUP
    query = lane % GROUP
    axial = (cell[:, None] // SIDE == query[None, :] // SIDE) + 1.0 * (
        (cell[:, None] == query[None, :]) & (slot[:, None] // GROUP == RANGE)
    )
    strips = np.zeros((2 * STRIP, CELLS), np.float32)
    for c in range(RAD):
        for r in range(SIDE):
            strips[c * SIDE + r, r * SIDE + SIDE - RAD + c] = 1
            strips[STRIP + c * SIDE + r, r * SIDE + c] = 1
    corners = np.zeros((2 * STRIP, 2 * STRIP), np.float32)
    for side in range(2):
        for c in range(RAD):
            for r in range(RAD):
                at = side * RAD * RAD + c * RAD + r
                corners[at, side * STRIP + c * SIDE + r] = 1
                corners[STRIP + at, side * STRIP + c * SIDE + SIDE - RAD + r] = 1
    parts = [np.concatenate([window[0], window[1]], axis=1), axial, strips, strips.T, corners, corners.T]
    return jnp.asarray(np.concatenate([np.pad(t, ((0, 0), (0, 256 - t.shape[1]))) for t in parts]), BF)


class Part:
    def __init__(self, ref, first, rows, lanes):
        self.ref, self.first, self.rows, self.lanes = ref, first, rows, lanes

    def read(self, first=0, rows=None, lane=0, lanes=None):
        start = self.first + first
        end = start + (self.rows - first if rows is None else rows)
        return self.ref[start:end, lane:lane + (self.lanes if lanes is None else lanes)]


def mm(a, b):
    return jnp.dot(a, b, preferred_element_type=F32)


def mm_nt(a, b):
    return lax.dot_general(a, b, (((1,), (1,)), ((), ())), preferred_element_type=F32)


def mm_tn(a, b):
    return lax.dot_general(a, b, (((0,), (0,)), ((), ())), preferred_element_type=F32)


def stacked_heads(block):
    low = lax.broadcasted_iota(jnp.int32, block.shape, 1) < HEAD
    zero = jnp.zeros_like(block)
    return jnp.concatenate([jnp.where(low, block, zero), jnp.where(low, zero, block)], axis=0)


def probabilities(scores, dprob):
    top = jnp.max(scores, axis=0, keepdims=True)
    expo = jnp.exp(scores - top)
    probs = expo * (1.0 / jnp.sum(expo, axis=0, keepdims=True))
    delta = jnp.sum(probs * dprob, axis=0, keepdims=True)
    return probs.astype(BF), (probs * (dprob - delta)).astype(BF)


def kernel(
    nlon, nlat,
    q_hbm, k_hbm, v_hbm, g_hbm, table_hbm, flag_ref, listed_ref,
    out_hbm, gq_hbm, gk_hbm, gv_hbm,
    out_ref, gq_ref, gk_ref, gv_ref, store_s,
    q_ref, k_ref, v_ref, g_ref, table_ref, load_s, flags, columns, bias, xbias, kv, strip_out, corner_out, xkv,
    acc, sides, edge_out, edge_in, side_out, side_in, gx, hop_out, hop_in,
    flag_s, flag_r, strip_s, strip_r, edge_s, edge_r, corner_s, corner_r, ax_s, ax_r,
    bedge_s, bedge_r, bside_s, bside_r, hop_s, hop_r,
):
    loads = [
        pltpu.make_async_copy(src, dst, load_s.at[i])
        for i, (src, dst) in enumerate(
            ((k_hbm, k_ref), (v_hbm, v_ref), (table_hbm, table_ref), (q_hbm, q_ref), (g_hbm, g_ref))
        )
    ]
    for load in loads:
        load.start()
    views = []
    at = 0
    for rows, lanes in ((KEYS, 256), (NSLOT * GROUP, 128), (2 * STRIP, 256), (CELLS, 192), (2 * STRIP, 192), (2 * STRIP, 192)):
        views.append(Part(table_ref, at, rows, lanes))
        at += rows
    near_ref, row_ref, strips_ref, strips_t_ref, corners_ref, corners_t_ref = views
    lon = lax.axis_index("lon")
    lat = lax.axis_index("lat")
    has_up = lat > 0
    has_down = lat < nlat - 1

    def device(dlon, dlat):
        return {"lon": lax.rem(lon + dlon + nlon, nlon), "lat": lax.rem(lat + dlat + nlat, nlat)}

    def remote(src, dst, send, recv, dlon, dlat):
        return pltpu.make_async_remote_copy(
            src_ref=src, dst_ref=dst, send_sem=send, recv_sem=recv,
            device_id=device(dlon, dlat), device_id_type=pl.DeviceIdType.MESH,
        )

    barrier = pltpu.get_barrier_semaphore()
    for dlon, dlat in NEAR:
        pl.semaphore_signal(barrier, inc=1, device_id=device(dlon, dlat), device_id_type=pl.DeviceIdType.MESH)

    flags[RANGE] = flag_ref[...]
    for tile, there in enumerate((has_up, has_down)):
        kv[tile, :, CORNER + TURN:KEYS] = jnp.zeros((2, KEYS - CORNER - TURN, WCH), BF)
        edge_in[tile, :, STRIP + TURN:] = jnp.zeros((2, STRIP - TURN, WCH), BF)

        @pl.when(jnp.logical_not(there))
        def _():
            kv[tile, :, EDGE:CORNER + TURN] = jnp.zeros((2, STRIP + TURN, WCH), BF)
            edge_in[tile, :, 0:STRIP + TURN] = jnp.zeros((2, STRIP + TURN, WCH), BF)

    for part, ref in enumerate((k_ref, v_ref)):
        loads[part].wait()
        for pair in range(XPAIRS):
            at = (2 * pair + part) * PAIR
            xkv[RANGE, :, at:at + PAIR] = ref[:, WCH + pair * PAIR:WCH + (pair + 1) * PAIR]
        kv[0, part, 0:CELLS] = ref[:, :WCH]

    pl.semaphore_wait(barrier, len(NEAR))

    def flag_copy(index):
        dlon, dlat = NEAR[index]
        slot = {0: RANGE, -1: 11, 1: 8}[dlat] - dlon
        return remote(flags.at[RANGE], flags.at[slot], flag_s.at[index], flag_r.at[slot], dlon, dlat)

    def strip_copy(way, piece):
        lanes = pl.ds(piece * WIDE, WIDE)
        return remote(
            strip_out.at[:, pl.ds(way * STRIP, STRIP), lanes], kv.at[0, :, pl.ds(LEFT + way * STRIP, STRIP), lanes],
            strip_s.at[way, piece], strip_r.at[way, piece], 1 - 2 * way, 0,
        )

    def edge_copy(way):
        return remote(
            kv.at[0, :, pl.ds(way * (CELLS - STRIP), STRIP)], kv.at[1 - way, :, pl.ds(EDGE, STRIP)],
            edge_s.at[way], edge_r.at[way], 0, 2 * way - 1,
        )

    def corner_copy(way, piece):
        lanes = pl.ds(pl.multiple_of(piece * WIDE, WIDE), WIDE)
        return remote(
            corner_out.at[:, pl.ds(way * STRIP, TURN), lanes], kv.at[1 - way, :, pl.ds(CORNER, TURN), lanes],
            corner_s.at[way, piece], corner_r.at[way, piece], 0, 2 * way - 1,
        )

    def ax_copy(way, step, pair):
        sign = 1 - 2 * way
        lanes = pl.ds(pair * 2 * PAIR, 2 * PAIR)
        return remote(
            xkv.at[RANGE - sign * step, :, lanes], xkv.at[RANGE - sign * (step + 1), :, lanes],
            ax_s.at[way, step, pair], ax_r.at[way, step, pair], sign, 0,
        )

    def edge_back(way, pair):
        lanes = pl.ds(pl.multiple_of(pair * PAIR, PAIR), PAIR)
        return remote(
            edge_out.at[way, :, pl.ds(0, STRIP + TURN), lanes], edge_in.at[1 - way, :, pl.ds(0, STRIP + TURN), lanes],
            bedge_s.at[way, pair], bedge_r.at[way, pair], 0, 2 * way - 1,
        )

    def side_back(way, pair):
        lanes = pl.ds(pl.multiple_of(pair * PAIR, PAIR), PAIR)
        rows = pl.ds(way * STRIP, STRIP)
        return remote(
            side_out.at[:, rows, lanes], side_in.at[:, rows, lanes],
            bside_s.at[way, pair], bside_r.at[way, pair], 2 * way - 1, 0,
        )

    def hop_back(way, step, pair):
        lanes = pl.ds(pair * 2 * PAIR, 2 * PAIR)
        return remote(
            hop_out.at[way, step, :, lanes], hop_in.at[way, step, :, lanes],
            hop_s.at[way, step, pair], hop_r.at[way, step, pair], 1 - 2 * way, 0,
        )

    def vertical(make, sending):
        @pl.when(has_up)
        def _():
            make(0 if sending else 1)

        @pl.when(has_down)
        def _():
            make(1 if sending else 0)

    def send_strips(piece):
        for way in range(2):
            strip_copy(way, piece).start()

    def turn_strips(piece):
        lanes = slice(piece * WIDE, (piece + 1) * WIDE)
        for way in range(2):
            strip_copy(way, piece).wait_recv()
        for part in range(2):
            strip = kv[0, part, LEFT:EDGE, lanes]
            kv[1, part, LEFT:EDGE, lanes] = strip
            corner_out[part, :, lanes] = mm(corners_ref.read(), strip).astype(BF)
        vertical(lambda way: corner_copy(way, piece).start(), True)

    for pair in range(XPAIRS):
        for way in range(2):
            ax_copy(way, 0, pair).start()
    vertical(lambda way: edge_copy(way).start(), True)
    for index in range(len(NEAR)):
        flag_copy(index).start()
    loads[2].wait()
    for part in range(2):
        strip_out[part] = mm(strips_ref.read(), kv[0, part, 0:CELLS]).astype(BF)
    send_strips(0)
    kv[1, :, 0:CELLS] = kv[0, :, 0:CELLS]

    for index in range(len(NEAR)):
        flag_copy(index).wait_recv()
    for slot in range(13):
        for half in range(2):
            row = jnp.broadcast_to(flags[slot, half:half + 1, :], (128, 128))
            columns[slot, half * 128:(half + 1) * 128] = row.T.astype(BF)

    def sides_of(left, right):
        return jnp.concatenate(
            [mm(strips_ref.read(0, STRIP), columns[left]), mm(strips_ref.read(STRIP), columns[right])], axis=0
        )

    own_flags = columns[RANGE].astype(F32)
    side_flags = sides_of(RANGE - 1, RANGE + 1)
    for tile, there in enumerate((has_up, has_down)):
        base = 7 + 3 * tile
        lives = jnp.where(there, 1.0, 0.0)
        first = CELLS - STRIP if tile == 0 else 0
        edge_flags = columns[base + 1, first:first + STRIP].astype(F32)
        turn = corners_ref.read(STRIP) if tile == 0 else corners_ref.read(0, STRIP)
        corner_flags = mm(turn, sides_of(base, base + 2).astype(BF))
        serves = jnp.concatenate([own_flags, side_flags, edge_flags * lives, corner_flags * lives], axis=0)
        bias[tile] = jnp.where(near_ref.read(lane=tile * 128, lanes=128).astype(F32) + serves > 1.5, 0.0, NEG)
    for group in range(GROUPS):
        serves = jnp.concatenate(
            [
                columns[slot, group * GROUP:(group + 1) * GROUP].astype(F32) * listed_ref[slot:slot + 1, :]
                for slot in range(NSLOT)
            ],
            axis=0,
        )
        xbias[group] = jnp.where(row_ref.read().astype(F32) + serves > 1.5, 0.0, NEG)

    def forward(step):
        for pair in range(XPAIRS):
            for way in range(2):
                ax_copy(way, step - 1, pair).wait_recv()
                ax_copy(way, step, pair).start()

    forward(1)
    for load in loads[3:]:
        load.wait()
    send_strips(1)
    turn_strips(0)
    forward(2)
    send_strips(2)

    def send_sides(pair):
        lanes = pl.ds(pl.multiple_of(pair * PAIR, PAIR), PAIR)
        vertical(lambda way: edge_back(way, pair).wait_recv(), False)
        for part in range(2):
            found = jnp.concatenate(
                [edge_in[0, part, STRIP:2 * STRIP, lanes], edge_in[1, part, STRIP:2 * STRIP, lanes]], axis=0
            )
            side_out[part, :, lanes] = (sides[part, :, lanes] + mm(corners_t_ref.read(), found)).astype(BF)
        for way in range(2):
            side_back(way, pair).start()

    def axial_pair(pair):
        for way in range(2):
            ax_copy(way, 2, pair).wait_recv()
        lanes = slice(WCH + pair * PAIR, WCH + (pair + 1) * PAIR)
        key_lanes = slice(2 * pair * PAIR, (2 * pair + 1) * PAIR)
        value_lanes = slice((2 * pair + 1) * PAIR, (2 * pair + 2) * PAIR)

        def axial_group(group, carry):
            cells = pl.ds(pl.multiple_of(group * GROUP, GROUP), GROUP)
            queries = stacked_heads(q_ref[cells, lanes] * jnp.asarray(SCALE, BF))
            cotangents = stacked_heads(g_ref[cells, lanes])
            keys = xkv[:, cells, key_lanes].reshape(NSLOT * GROUP, PAIR)
            values = xkv[:, cells, value_lanes].reshape(NSLOT * GROUP, PAIR)
            scores = mm_nt(keys, queries) + xbias[group]
            probs, dscore = probabilities(scores, mm_nt(values, cotangents))
            attended = mm_tn(probs, values)
            grad_q = mm_tn(dscore, keys)
            low = lax.broadcasted_iota(jnp.int32, (GROUP, PAIR), 1) < HEAD
            out_ref[cells, lanes] = jnp.where(low, attended[0:GROUP], attended[GROUP:]).astype(BF)
            gq_ref[cells, lanes] = (jnp.where(low, grad_q[0:GROUP], grad_q[GROUP:]) * SCALE).astype(BF)
            gx[:, cells, key_lanes] = mm(dscore, queries).reshape(NSLOT, GROUP, PAIR)
            gx[:, cells, value_lanes] = mm(probs, cotangents).reshape(NSLOT, GROUP, PAIR)
            return carry

        lax.fori_loop(0, GROUPS, axial_group, 0)
        both = slice(2 * pair * PAIR, (2 * pair + 2) * PAIR)
        for way in range(2):
            hop_out[way, 0, :, both] = gx[2 * RANGE * (1 - way), :, both].astype(BF)
            hop_back(way, 0, pair).start()

    def hop(step):
        for pair in range(XPAIRS):
            both = slice(2 * pair * PAIR, (2 * pair + 2) * PAIR)
            for way in range(2):
                slot = 2 * RANGE - step if way == 0 else step
                hop_back(way, step - 1, pair).wait_recv()
                total = gx[slot, :, both] + hop_in[way, step - 1, :, both].astype(F32)
                hop_out[way, step, :, both] = total.astype(BF)
                hop_back(way, step, pair).start()

    def window_pair(pair, carry):
        lanes = pl.ds(pl.multiple_of(pair * PAIR, PAIR), PAIR)

        @pl.when(lax.rem(pair, WIDE // PAIR) == 0)
        def _():
            vertical(lambda way: corner_copy(way, pair // (WIDE // PAIR)).wait_recv(), False)

        grads = []
        for tile in range(2):
            rows = slice(tile * 128, (tile + 1) * 128)
            queries = stacked_heads(q_ref[rows, lanes] * jnp.asarray(SCALE, BF))
            cotangents = stacked_heads(g_ref[rows, lanes])
            keys = kv[tile, 0, :, lanes]
            values = kv[tile, 1, :, lanes]
            penalty = bias[tile]
            scores = mm_nt(keys, queries) + jnp.concatenate([penalty, penalty], axis=1)
            probs, dscore = probabilities(scores, mm_nt(values, cotangents))
            attended = mm_tn(values, probs)
            grad_q = mm_tn(keys, dscore)
            for result, ref, factor in ((attended, out_ref, 1.0), (grad_q, gq_ref, SCALE)):
                both = jnp.concatenate([result[0:HEAD, 0:128], result[HEAD:, 128:]], axis=0)
                ref[rows, lanes] = (both.T * factor).astype(BF)
            grads.append((mm(dscore, queries), mm(probs, cotangents)))
        for part in range(2):
            first, second = grads[0][part], grads[1][part]
            acc[part, :, lanes] = first[0:CELLS] + second[0:CELLS]
            sides[part, :, lanes] = first[LEFT:EDGE] + second[LEFT:EDGE]
            edge_out[0, part, :, lanes] = first[EDGE:].astype(BF)
            edge_out[1, part, :, lanes] = second[EDGE:].astype(BF)
        vertical(lambda way: edge_back(way, pair).start(), True)

        for step in range(1, RANGE):
            @pl.when(pair == 2 * step)
            def _():
                hop(step)

        @pl.when(pair >= LAG)
        def _():
            send_sides(pair - LAG)

        return carry

    for pair in range(XPAIRS):
        axial_pair(pair)
        turn_strips(1 + pair)
    vertical(lambda way: edge_copy(way).wait_recv(), False)
    lax.fori_loop(0, PAIRS, window_pair, 0)
    stores = [
        pltpu.make_async_copy(src, dst, store_s.at[i])
        for i, (src, dst) in enumerate(
            ((out_ref, out_hbm), (gq_ref, gq_hbm), (gk_ref, gk_hbm), (gv_ref, gv_hbm))
        )
    ]
    for store in stores[:2]:
        store.start()
    for late in range(LAG):
        send_sides(PAIRS - LAG + late)

    for pair in range(XPAIRS):
        lanes = slice(WCH + pair * PAIR, WCH + (pair + 1) * PAIR)
        for way in range(2):
            hop_back(way, RANGE - 1, pair).wait_recv()
        for part, ref in enumerate((gk_ref, gv_ref)):
            at = slice((2 * pair + part) * PAIR, (2 * pair + part + 1) * PAIR)
            total = gx[RANGE, :, at]
            for way in range(2):
                total = total + hop_in[way, RANGE - 1, :, at].astype(F32)
            ref[:, lanes] = total.astype(BF)

    for piece in range(PIECES):
        lanes = slice(piece * WIDE, (piece + 1) * WIDE)
        for pair in range(piece * (WIDE // PAIR), (piece + 1) * (WIDE // PAIR)):
            for way in range(2):
                side_back(way, pair).wait_recv()
        for part, ref in enumerate((gk_ref, gv_ref)):
            total = acc[part, :, lanes] + mm(strips_t_ref.read(), side_in[part, :, lanes])
            top = total[0:STRIP] + edge_in[0, part, 0:STRIP, lanes].astype(F32)
            bottom = total[CELLS - STRIP:] + edge_in[1, part, 0:STRIP, lanes].astype(F32)
            ref[0:STRIP, lanes] = top.astype(BF)
            ref[STRIP:CELLS - STRIP, lanes] = total[STRIP:CELLS - STRIP].astype(BF)
            ref[CELLS - STRIP:, lanes] = bottom.astype(BF)

    for store in stores[2:]:
        store.start()

    for index in range(len(NEAR)):
        flag_copy(index).wait_send()
    for way in range(2):
        for piece in range(PIECES):
            strip_copy(way, piece).wait_send()
        for step in range(RANGE):
            for pair in range(XPAIRS):
                ax_copy(way, step, pair).wait_send()
                hop_back(way, step, pair).wait_send()
        for pair in range(PAIRS):
            side_back(way, pair).wait_send()
    vertical(lambda way: edge_copy(way).wait_send(), True)
    for piece in range(PIECES):
        vertical(lambda way: corner_copy(way, piece).wait_send(), True)
    for pair in range(PAIRS):
        vertical(lambda way: edge_back(way, pair).wait_send(), True)
    for store in stores:
        store.wait()


def store_kernel(*refs):
    count = len(refs) // 2
    sources, targets, done = refs[:count], refs[count:2 * count], refs[-1]
    copies = [
        pltpu.make_async_copy(src, dst, done.at[i]) for i, (src, dst) in enumerate(zip(sources, targets))
    ]
    for copy in copies:
        copy.start()
    for copy in copies:
        copy.wait()


def per_device(nlon, nlat, queries, key_vectors, value_vectors, grad_out, key_mask, block_lists):
    shape = queries.shape
    flat = [x.reshape(CELLS, shape[-1]) for x in (queries, key_vectors, value_vectors, grad_out)]
    flag = jnp.pad((key_mask > 0).astype(F32).reshape(2, 128), ((0, 6), (0, 0)))
    offset = (block_lists[0] - lax.axis_index("lon") + RANGE + nlon) % nlon
    listed = jnp.any(jnp.arange(8)[:, None] == offset[None, :], axis=1)
    listed = jnp.broadcast_to(listed[:, None], (8, 128)).astype(F32)
    table = tables()
    vmem = pl.BlockSpec(memory_space=pltpu.VMEM)
    dma = lambda *s: pltpu.SemaphoreType.DMA(s)
    outs = pl.pallas_call(
        functools.partial(kernel, nlon, nlat),
        out_shape=[jax.ShapeDtypeStruct((CELLS, shape[-1]), BF)] * 4,
        in_specs=[pl.BlockSpec(memory_space=pltpu.HBM)] * 5 + [vmem] * 2,
        out_specs=[pl.BlockSpec(memory_space=pltpu.HBM)] * 4,
        scratch_shapes=[
            *[pltpu.VMEM((CELLS, shape[-1]), BF)] * 4,
            dma(4),
            *[pltpu.VMEM((CELLS, shape[-1]), BF)] * 4,
            pltpu.VMEM(table.shape, BF),
            dma(5),
            pltpu.VMEM((13, 8, 128), F32),
            pltpu.VMEM((13, CELLS, 128), BF),
            pltpu.VMEM((2, KEYS, 128), F32),
            pltpu.VMEM((GROUPS, NSLOT * GROUP, 128), F32),
            pltpu.VMEM((2, 2, KEYS, WCH), BF),
            pltpu.VMEM((2, 2 * STRIP, WCH), BF),
            pltpu.VMEM((2, 2 * STRIP, WCH), BF),
            pltpu.VMEM((NSLOT, CELLS, 2 * XPAIRS * PAIR), BF),
            pltpu.VMEM((2, CELLS, WCH), F32),
            pltpu.VMEM((2, 2 * STRIP, WCH), F32),
            pltpu.VMEM((2, 2, 2 * STRIP, WCH), BF),
            pltpu.VMEM((2, 2, 2 * STRIP, WCH), BF),
            pltpu.VMEM((2, 2 * STRIP, WCH), BF),
            pltpu.VMEM((2, 2 * STRIP, WCH), BF),
            pltpu.VMEM((NSLOT, CELLS, 2 * XPAIRS * PAIR), F32),
            pltpu.VMEM((2, RANGE, CELLS, 2 * XPAIRS * PAIR), BF),
            pltpu.VMEM((2, RANGE, CELLS, 2 * XPAIRS * PAIR), BF),
            dma(len(NEAR)), dma(13), dma(2, PIECES), dma(2, PIECES), dma(2), dma(2), dma(2, PIECES), dma(2, PIECES),
            dma(2, RANGE, XPAIRS), dma(2, RANGE, XPAIRS), dma(2, PAIRS), dma(2, PAIRS), dma(2, PAIRS), dma(2, PAIRS),
            dma(2, RANGE, XPAIRS), dma(2, RANGE, XPAIRS),
        ],
        compiler_params=pltpu.CompilerParams(
            collective_id=0, has_side_effects=True, vmem_limit_bytes=52 * 1024 * 1024
        ),
        cost_estimate=pl.CostEstimate(flops=4_000_000_000, bytes_accessed=5_000_000, transcendentals=3_000_000),
    )(*flat, table, flag, listed)
    stored = pl.pallas_call(
        store_kernel,
        out_shape=[jax.ShapeDtypeStruct((CELLS, shape[-1]), BF)] * 4,
        in_specs=[pl.BlockSpec(memory_space=pltpu.HBM)] * 4,
        out_specs=[pl.BlockSpec(memory_space=pltpu.HBM)] * 4,
        scratch_shapes=[dma(4)],
        compiler_params=pltpu.CompilerParams(vmem_limit_bytes=1024 * 1024),
        cost_estimate=pl.CostEstimate(flops=0, bytes_accessed=4_000_000, transcendentals=0),
    )(*outs)
    return tuple(x.reshape(shape) for x in stored)


def solution(mesh):
    cells = P("lat", "lon", None)
    return jax.shard_map(
        functools.partial(per_device, mesh.shape["lon"], mesh.shape["lat"]),
        mesh=mesh,
        in_specs=(cells, cells, cells, cells, P("lat", "lon"), P("lon", None)),
        out_specs=(cells, cells, cells, cells),
        check_vma=False,
    )
```
